128 devices in a mesh: depth: 8 (over y, core), tile: 16 (over z, x).
Axes of the slice: x: 4, y: 4, z: 4, core: 2. Of those that a mesh axis runs over, the one named last changes fastest.
Arguments:
- velocity: float32 [3, 256, 256, 1024], P(None, 'depth', 'tile'), may hold values from -6 to 6
- sigma_table: float32 [16], replicated, may hold values from 0.5 to 6
- color_table: float32 [3, 16], replicated, may hold values from 0.05 to 1
Outputs:
- image: float32 [4, 256, 1024], P(None, 'tile', 'depth')
The draws below stay inside these ranges and needn't reach their ends.
All inputs are finite; a program needn't handle non-finite values.
Results may differ from the reference program's by a relative error of at most 0.0003.
Values sent between devices are 32-bit elements; how exact they have to be, the bound alone decides.
No kernel may reach another device: no remote copies, remote signals or barrier semaphores. Data moves between devices by JAX's collectives and lax.ppermute only.
A program may use at most 128 MiB of HBM per device.

```python
import math
import jax
import jax.numpy as jnp
from jax import lax

NY = 1024
BINS = 16
NX = 256
NZ = 256


def block_levels(own_key, extent, cuts, low, largest):
    gain, own = 1.0, jax.random.fold_in(own_key, 6)
    for dim, parts in cuts:
        steps = jnp.exp(jax.random.uniform(jax.random.fold_in(own, dim), (parts,), jnp.float32, low / len(cuts), largest / len(cuts)))
        gain = gain * jnp.repeat(steps, extent[dim] // parts).reshape([-1 if axis == dim else 1 for axis in range(len(extent))])
    return gain


def noise(rng, dims, width, most, split=(), kind=jnp.bfloat16):
    drawn = width * jax.random.normal(rng, dims, jnp.float32)
    if split:
        drawn = drawn * block_levels(rng, dims, split, -0.22, 0.18)
    return jnp.clip(drawn, -most, most).astype(kind)


def setup_inputs(seed: int = 0) -> dict:
    arg_keys = jax.random.split(jax.random.key(seed), 4)
    velocity = noise(arg_keys[0], (3, NZ, NX, NY), 1.0, 6.0, ((1, 8), (2, 16)), jnp.float32)
    sigma_table = jnp.clip(jnp.exp(jax.random.uniform(arg_keys[1], (BINS,), jnp.float32, math.log(0.5), math.log(6.0))), 0.5, 6.0)
    color_table = jnp.clip(jax.random.uniform(arg_keys[2], (3, BINS), jnp.float32, 0.05, 1.0), 0.05, 1.0)
    return dict(velocity=velocity, sigma_table=sigma_table, color_table=color_table)


def stencil_axis(field, axis):
    count = field.shape[axis]
    widths = [(0, 0)] * field.ndim
    widths[axis] = (2, 2)
    padded = jnp.pad(field, widths)
    far_hi = lax.slice_in_dim(padded, 4, count + 4, axis=axis)
    near_hi = lax.slice_in_dim(padded, 3, count + 3, axis=axis)
    near_lo = lax.slice_in_dim(padded, 1, count + 1, axis=axis)
    far_lo = lax.slice_in_dim(padded, 0, count, axis=axis)
    return (-far_hi + 8.0 * near_hi - 8.0 * near_lo + far_lo) / 12.0


def transfer(qcrit, sigma_table, color_table, depth_total):
    pos = (sigma_table.shape[0] - 1) * jax.nn.sigmoid(qcrit / 2.0)
    tau = jnp.zeros_like(qcrit)
    colors = jnp.zeros((3,) + qcrit.shape, jnp.float32)
    for entry in range(sigma_table.shape[0]):
        hat = jnp.maximum(0.0, 1.0 - jnp.abs(pos - entry))
        tau = tau + sigma_table[entry] * hat
        colors = colors + color_table[:, entry][:, None, None] * hat[None]
    return tau / depth_total, colors


def reference(velocity, sigma_table, color_table):
    depth_total = velocity.shape[1]

    def layer(carry, zpos):
        optical, shade = carry
        slabs = []
        for offset in range(-2, 3):
            where = zpos + offset
            clamped = jnp.clip(where, 0, depth_total - 1).astype(jnp.int32)
            inside = ((where >= 0) & (where < depth_total)).astype(jnp.float32)
            piece = lax.dynamic_slice_in_dim(velocity, clamped, 1, 1)[:, 0]
            slabs.append(piece * inside)
        dz = (-slabs[4] + 8.0 * slabs[3] - 8.0 * slabs[1] + slabs[0]) / 12.0
        center = slabs[2]
        dx = stencil_axis(center, 1)
        dy = stencil_axis(center, 2)
        grads = [dz, dx, dy]
        qcrit = jnp.zeros(center.shape[1:], jnp.float32)
        for comp in range(3):
            for direc in range(3):
                qcrit = qcrit + grads[direc][comp] * grads[comp][direc]
        qcrit = -0.5 * qcrit
        tau, colors = transfer(qcrit, sigma_table, color_table, depth_total)
        alpha = 1.0 - jnp.exp(-tau)
        shade = shade + (jnp.exp(-optical) * alpha)[None] * colors
        optical = optical + tau
        return (optical, shade), None

    start = (jnp.zeros(velocity.shape[2:], jnp.float32), jnp.zeros((3,) + velocity.shape[2:], jnp.float32))
    (optical, shade), _ = lax.scan(layer, start, jnp.arange(depth_total, dtype=jnp.int32))
    return jnp.concatenate([shade, jnp.exp(-optical)[None]], axis=0)
```

```python
import functools

import jax
import jax.numpy as jnp
from jax import lax
from jax.experimental import pallas as pl
from jax.experimental.pallas import tpu as pltpu
from jax.sharding import PartitionSpec as P

F32 = jnp.float32
VMEM_LIMIT = 40 * 1024 * 1024
QSCALE = -1.0 / 1152.0


def shift_up(count):
    return [(i, i + 1) for i in range(count - 1)]


def shift_down(count):
    return [(i + 1, i) for i in range(count - 1)]


def pack_kernel(v_ref, up_ref, down_ref, zup_ref, zdown_ref):
    zdown_ref[...] = v_ref[:, 0:2]
    zup_ref[...] = v_ref[:, 30:32]
    row = lax.broadcasted_iota(jnp.int32, (8, 1024), 0)
    for quarter in range(4):
        for zz in range(8):
            z = quarter * 8 + zz
            low = v_ref[0, z, 0:8, :]
            high = v_ref[0, z, 8:16, :]
            up = jnp.where(row == 6, high - 8.0 * pltpu.roll(high, 7, 0), high)
            down = jnp.where(row == 0, -low, 8.0 * pltpu.roll(low, 1, 0) - low)
            up_ref[0, zz, 2 * quarter : 2 * quarter + 2, :] = up[6:8]
            down_ref[0, zz, 2 * quarter : 2 * quarter + 2, :] = down[0:2]


def pack(velocity):
    comps, depth, width, length = velocity.shape
    ends = jax.ShapeDtypeStruct((comps, 8, 8, length), F32)
    layers = jax.ShapeDtypeStruct((comps, 2, width, length), F32)
    block = lambda *shape: pl.BlockSpec((1,) + shape, lambda c: (c, 0, 0, 0))
    return pl.pallas_call(
        pack_kernel,
        grid=(comps,),
        in_specs=[block(depth, width, length)],
        out_specs=[block(8, 8, length)] * 2 + [block(2, width, length)] * 2,
        out_shape=[ends, ends, layers, layers],
        compiler_params=pltpu.CompilerParams(vmem_limit_bytes=VMEM_LIMIT),
        cost_estimate=pl.CostEstimate(flops=2000000, bytes_accessed=9000000, transcendentals=0),
        name="pack",
    )(velocity)


def lookup(qcrit, tables):
    pos = 7.5 * jnp.tanh(qcrit) + 7.5
    index = jnp.minimum(pos.astype(jnp.int32), 14)
    base = [jnp.take_along_axis(t, index, axis=1, mode="promise_in_bounds") for t in tables]
    vals = [base[k] + base[k + 4] * pos for k in range(4)]
    return jnp.exp(vals[0]), vals[1:]


def composite(carry, step, colors):
    trans, shades = carry
    after = trans * step
    weight = trans - after
    return after, [s + weight * c for s, c in zip(shades, colors)]


def main_kernel(v_hbm, zlo_hbm, zhi_hbm, tab_ref, comp_ref, edge_ref, buf, sems):
    j = pl.program_id(0)

    def copies(k):
        lanes = pl.ds(pl.multiple_of(k * 128, 128), 128)
        inner = pl.ds(pl.multiple_of((k + 1) * 128, 128), 128)
        return [
            pltpu.make_async_copy(v_hbm.at[:, :, :, lanes], buf.at[:, 2:34, :, inner], sems.at[0, k]),
            pltpu.make_async_copy(zlo_hbm.at[:, :, :, lanes], buf.at[:, 0:2, :, inner], sems.at[1, k]),
            pltpu.make_async_copy(zhi_hbm.at[:, :, :, lanes], buf.at[:, 34:36, :, inner], sems.at[2, k]),
        ]

    @pl.when(j == 0)
    def _():
        for k in range(8):
            for copy in copies(k):
                copy.start()
        zeros = jnp.zeros((3, 36, 16, 128), F32)
        buf[:, :, :, 0:128] = zeros
        buf[:, :, :, 9 * 128 : 10 * 128] = zeros
        for copy in copies(0):
            copy.wait()

    @pl.when(j < 7)
    def _():
        for copy in copies(j + 1):
            copy.wait()

    row = lax.broadcasted_iota(jnp.int32, (16, 128), 0)
    lane = lax.broadcasted_iota(jnp.int32, (16, 128), 1)
    tables = [jnp.broadcast_to(tab_ref[k : k + 1, :], (16, 128)) for k in range(8)]
    left = pl.ds(pl.multiple_of(j * 128, 128), 128)
    mid = pl.ds(pl.multiple_of(j * 128 + 128, 128), 128)
    right = pl.ds(pl.multiple_of(j * 128 + 256, 128), 128)

    def layer(quarter, zz, carry):
        z = quarter * 8 + zz
        dz, dx, dy = [], [], []
        for c in range(3):
            center = buf[c, z + 2, :, mid]
            dz.append(8.0 * (buf[c, z + 3, :, mid] - buf[c, z + 1, :, mid]) - (buf[c, z + 4, :, mid] - buf[c, z, :, mid]))
            p1 = jnp.where(row < 15, pltpu.roll(center, 15, 0), 0.0)
            m1 = jnp.where(row > 0, pltpu.roll(center, 1, 0), 0.0)
            p2 = jnp.where(row < 14, pltpu.roll(center, 14, 0), 0.0)
            m2 = jnp.where(row > 1, pltpu.roll(center, 2, 0), 0.0)
            dx.append(8.0 * (p1 - m1) - (p2 - m2))
            lo = buf[c, z + 2, :, left]
            hi = buf[c, z + 2, :, right]
            p1 = pltpu.roll(jnp.where(lane < 1, hi, center), 127, 1)
            m1 = pltpu.roll(jnp.where(lane > 126, lo, center), 1, 1)
            p2 = pltpu.roll(jnp.where(lane < 2, hi, center), 126, 1)
            m2 = pltpu.roll(jnp.where(lane > 125, lo, center), 2, 1)
            dy.append(8.0 * (p1 - m1) - (p2 - m2))
        cross = dz[1] * dx[0] + dz[2] * dy[0] + dx[2] * dy[1]
        total = dz[0] * dz[0] + dx[1] * dx[1] + dy[2] * dy[2] + 2.0 * cross
        for e, value in enumerate((total, 2.0 * dz[1], 2.0 * dx[1], 2.0 * dy[1])):
            edge_ref[e, 0, zz, 2 * quarter : 2 * quarter + 2, :] = value[0:2]
            edge_ref[e, 1, zz, 2 * quarter : 2 * quarter + 2, :] = value[14:16]
        step, colors = lookup(QSCALE * total, tables)
        return composite(carry, step, colors)

    carry = (jnp.ones((16, 128), F32), [jnp.zeros((16, 128), F32)] * 3)
    for quarter in range(4):
        carry = lax.fori_loop(0, 8, functools.partial(layer, quarter), carry)
    for c in range(3):
        comp_ref[c] = carry[1][c]
    comp_ref[3] = carry[0]


def main_pass(velocity, before, after, table):
    comps, depth, width, length = velocity.shape
    hbm = pl.BlockSpec(memory_space=pl.ANY)
    return pl.pallas_call(
        main_kernel,
        grid=(8,),
        in_specs=[hbm, hbm, hbm, pl.BlockSpec((8, 128), lambda j: (0, 0))],
        out_specs=[
            pl.BlockSpec((4, width, 128), lambda j: (0, 0, j)),
            pl.BlockSpec((4, 2, 8, 8, 128), lambda j: (0, 0, 0, 0, j)),
        ],
        out_shape=[
            jax.ShapeDtypeStruct((4, width, length), F32),
            jax.ShapeDtypeStruct((4, 2, 8, 8, length), F32),
        ],
        scratch_shapes=[pltpu.VMEM((comps, depth + 4, width, length + 256), F32), pltpu.SemaphoreType.DMA((3, 8))],
        compiler_params=pltpu.CompilerParams(vmem_limit_bytes=VMEM_LIMIT),
        cost_estimate=pl.CostEstimate(flops=60000000, bytes_accessed=10000000, transcendentals=1000000),
        name="main_pass",
    )(velocity, before, after, table)


def edge_kernel(edge_ref, lo_ref, hi_ref, comp_ref, tab_ref, out_ref):
    tables = [jnp.broadcast_to(tab_ref[k : k + 1, :], (8, 128)) for k in range(8)]
    for half in range(2):
        lanes = slice(half * 128, half * 128 + 128)
        out_ref[half] = comp_ref[:, :, lanes]
        for side, halo_ref in enumerate((lo_ref, hi_ref)):
            carry = (jnp.ones((8, 128), F32), [jnp.zeros((8, 128), F32)] * 3)
            for zz in range(8):
                part, by_z, by_x, by_y = [edge_ref[e, side, zz, :, lanes] for e in range(4)]
                hz, hx, hy = [halo_ref[c, zz, :, lanes] for c in range(3)]
                total = part + by_z * hz + by_y * hy + hx * (by_x + hx)
                step, colors = lookup(QSCALE * total, tables)
                carry = composite(carry, step, colors)
            trans, shades = carry
            for _ in range(2):
                back = 2 if _ == 0 else 4
                behind = pltpu.roll(trans, 8 - back, 0)
                shades = [s + trans * pltpu.roll(s, 8 - back, 0) for s in shades]
                trans = trans * behind
            start = 14 * side
            for c in range(3):
                out_ref[half, c, start : start + 2, :] = shades[c][0:2]
            out_ref[half, 3, start : start + 2, :] = trans[0:2]


def edge_pass(edge, lo, hi, comp, table):
    length = comp.shape[2]
    width = comp.shape[1]
    halo = pl.BlockSpec((3, 8, 8, 256), lambda j: (0, 0, 0, j))
    return pl.pallas_call(
        edge_kernel,
        grid=(length // 256,),
        in_specs=[
            pl.BlockSpec((4, 2, 8, 8, 256), lambda j: (0, 0, 0, 0, j)),
            halo,
            halo,
            pl.BlockSpec((4, width, 256), lambda j: (0, 0, j)),
            pl.BlockSpec((8, 128), lambda j: (0, 0)),
        ],
        out_specs=pl.BlockSpec((2, 4, width, 128), lambda j: (j, 0, 0, 0)),
        out_shape=jax.ShapeDtypeStruct((8, 4, width, 128), F32),
        compiler_params=pltpu.CompilerParams(vmem_limit_bytes=VMEM_LIMIT),
        cost_estimate=pl.CostEstimate(flops=10000000, bytes_accessed=4000000, transcendentals=300000),
        name="edge_pass",
    )(edge, lo, hi, comp, table)


def over_kernel(parts_ref, out_ref):
    shades = [parts_ref[7, c] for c in range(3)]
    trans = parts_ref[7, 3]
    for layer in range(6, -1, -1):
        front = parts_ref[layer, 3]
        shades = [parts_ref[layer, c] + front * s for c, s in enumerate(shades)]
        trans = trans * front
    for c in range(3):
        out_ref[c] = shades[c]
    out_ref[3] = trans


def over(parts):
    return pl.pallas_call(
        over_kernel,
        out_shape=jax.ShapeDtypeStruct(parts.shape[1:], F32),
        name="over",
    )(parts)


def make_table(sigma_table, color_table, depth_total):
    values = jnp.concatenate([sigma_table[None] * (-1.0 / depth_total), color_table], axis=0)
    slopes = values[:, 1:] - values[:, :-1]
    starts = values[:, :-1] - slopes * jnp.arange(15, dtype=F32)
    table = jnp.concatenate([starts, slopes], axis=0)
    return jnp.pad(table, ((0, 0), (0, 113)))


def local(velocity, sigma_table, color_table):
    layers, tiles = lax.axis_size("depth"), lax.axis_size("tile")
    table = make_table(sigma_table, color_table, velocity.shape[1] * layers)
    up, down, zup, zdown = pack(velocity)
    lo = lax.ppermute(up, "tile", shift_up(tiles))
    hi = lax.ppermute(down, "tile", shift_down(tiles))
    before = lax.ppermute(zup, "depth", shift_up(layers))
    after = lax.ppermute(zdown, "depth", shift_down(layers))
    comp, edge = main_pass(velocity, before, after, table)
    pieces = edge_pass(edge, lo, hi, comp, table)
    received = lax.all_to_all(pieces, "depth", split_axis=0, concat_axis=0, tiled=True)
    return over(received)


def solution(mesh):
    return jax.shard_map(
        local,
        mesh=mesh,
        in_specs=(P(None, "depth", "tile", None), P(), P()),
        out_specs=P(None, "tile", "depth"),
        check_vma=False,
    )
```

```python
import functools

import jax
import jax.numpy as jnp
from jax import lax
from jax.experimental import pallas as pl
from jax.experimental.pallas import tpu as pltpu
from jax.sharding import PartitionSpec as P

F32 = jnp.float32
VMEM_LIMIT = 40 * 1024 * 1024
QSCALE = -1.0 / 1152.0


def shift_up(count):
    return [(i, i + 1) for i in range(count - 1)]


def shift_down(count):
    return [(i + 1, i) for i in range(count - 1)]


def pack_kernel(v_ref, up_ref, down_ref, zup_ref, zdown_ref):
    zdown_ref[...] = v_ref[:, 0:2]
    zup_ref[...] = v_ref[:, 30:32]
    row = lax.broadcasted_iota(jnp.int32, (8, 1024), 0)
    for quarter in range(4):
        for zz in range(8):
            z = quarter * 8 + zz
            low = v_ref[0, z, 0:8, :]
            high = v_ref[0, z, 8:16, :]
            up = jnp.where(row == 6, high - 8.0 * pltpu.roll(high, 7, 0), high)
            down = jnp.where(row == 0, -low, 8.0 * pltpu.roll(low, 1, 0) - low)
            up_ref[0, zz, 2 * quarter : 2 * quarter + 2, :] = up[6:8]
            down_ref[0, zz, 2 * quarter : 2 * quarter + 2, :] = down[0:2]


def pack(velocity):
    comps, depth, width, length = velocity.shape
    ends = jax.ShapeDtypeStruct((comps, 8, 8, length), F32)
    layers = jax.ShapeDtypeStruct((comps, 2, width, length), F32)
    block = lambda *shape: pl.BlockSpec((1,) + shape, lambda c: (c, 0, 0, 0))
    return pl.pallas_call(
        pack_kernel,
        grid=(comps,),
        in_specs=[block(depth, width, length)],
        out_specs=[block(8, 8, length)] * 2 + [block(2, width, length)] * 2,
        out_shape=[ends, ends, layers, layers],
        compiler_params=pltpu.CompilerParams(vmem_limit_bytes=VMEM_LIMIT),
        cost_estimate=pl.CostEstimate(flops=2000000, bytes_accessed=9000000, transcendentals=0),
        name="pack",
    )(velocity)


def lookup(qcrit, tab_ref):
    pos = 7.5 * jnp.tanh(qcrit) + 7.5
    index = jnp.minimum(pos.astype(jnp.int32), 14)
    low, index = index < 8, index & 7
    pick = lambda k: jnp.take_along_axis(tab_ref[k], index, axis=0, mode="promise_in_bounds")
    base = [jnp.where(low, pick(2 * k), pick(2 * k + 1)) for k in range(8)]
    vals = [base[k] + base[k + 4] * pos for k in range(4)]
    return jnp.exp(vals[0]), vals[1:]


def composite(carry, step, colors):
    trans, shades = carry
    after = trans * step
    weight = trans - after
    return after, [s + weight * c for s, c in zip(shades, colors)]


def main_kernel(v_hbm, zlo_hbm, zhi_hbm, tab_ref, comp_ref, edge_ref, buf, sems):
    j = pl.program_id(0)

    def copies(k):
        lanes = pl.ds(pl.multiple_of(k * 128, 128), 128)
        inner = pl.ds(pl.multiple_of((k + 1) * 128, 128), 128)
        return [
            pltpu.make_async_copy(v_hbm.at[:, :, :, lanes], buf.at[:, 2:34, :, inner], sems.at[0, k]),
            pltpu.make_async_copy(zlo_hbm.at[:, :, :, lanes], buf.at[:, 0:2, :, inner], sems.at[1, k]),
            pltpu.make_async_copy(zhi_hbm.at[:, :, :, lanes], buf.at[:, 34:36, :, inner], sems.at[2, k]),
        ]

    @pl.when(j == 0)
    def _():
        for k in range(8):
            for copy in copies(k):
                copy.start()
        zeros = jnp.zeros((3, 36, 16, 128), F32)
        buf[:, :, :, 0:128] = zeros
        buf[:, :, :, 9 * 128 : 10 * 128] = zeros
        for copy in copies(0):
            copy.wait()

    @pl.when(j < 7)
    def _():
        for copy in copies(j + 1):
            copy.wait()

    row = lax.broadcasted_iota(jnp.int32, (8, 128), 0)
    lane = lax.broadcasted_iota(jnp.int32, (8, 128), 1)
    left = pl.ds(pl.multiple_of(j * 128, 128), 128)
    mid = pl.ds(pl.multiple_of(j * 128 + 128, 128), 128)
    right = pl.ds(pl.multiple_of(j * 128 + 256, 128), 128)

    def layer(side, quarter, zz, z, window, carry):
        rows = slice(8 * side, 8 * side + 8)
        others = slice(8 - 8 * side, 16 - 8 * side)
        dz, dx, dy = [], [], []
        for c in range(3):
            w = window[c]
            center = w[2]
            dz.append(8.0 * (w[3] - w[1]) - (w[4] - w[0]))
            other = buf[c, z + 2, others, mid]
            above, below = (0.0, other) if side == 0 else (other, 0.0)
            p1 = pltpu.roll(jnp.where(row < 1, below, center), 7, 0)
            m1 = pltpu.roll(jnp.where(row > 6, above, center), 1, 0)
            p2 = pltpu.roll(jnp.where(row < 2, below, center), 6, 0)
            m2 = pltpu.roll(jnp.where(row > 5, above, center), 2, 0)
            dx.append(8.0 * (p1 - m1) - (p2 - m2))
            lo = buf[c, z + 2, rows, left]
            hi = buf[c, z + 2, rows, right]
            p1 = pltpu.roll(jnp.where(lane < 1, hi, center), 127, 1)
            m1 = pltpu.roll(jnp.where(lane > 126, lo, center), 1, 1)
            p2 = pltpu.roll(jnp.where(lane < 2, hi, center), 126, 1)
            m2 = pltpu.roll(jnp.where(lane > 125, lo, center), 2, 1)
            dy.append(8.0 * (p1 - m1) - (p2 - m2))
        cross = dz[1] * dx[0] + dz[2] * dy[0] + dx[2] * dy[1]
        total = dz[0] * dz[0] + dx[1] * dx[1] + dy[2] * dy[2] + 2.0 * cross
        ends = slice(6 * side, 6 * side + 2)
        for e, value in enumerate((total, 2.0 * dz[1], 2.0 * dx[1], 2.0 * dy[1])):
            edge_ref[e, side, zz, 2 * quarter : 2 * quarter + 2, :] = value[ends]
        step, colors = lookup(QSCALE * total, tab_ref)
        return composite(carry, step, colors)

    for side in range(2):
        rows = slice(8 * side, 8 * side + 8)
        zeros = jnp.zeros((8, 128), F32)
        carry = (zeros + 1.0, [zeros] * 3)
        for quarter in range(4):
            first = quarter * 8
            lines = [[buf[c, first + i, rows, mid] for i in range(12)] for c in range(3)]
            for i in range(8):
                window = [lines[c][i : i + 5] for c in range(3)]
                carry = layer(side, quarter, i, first + i, window, carry)
        for c in range(3):
            comp_ref[c, rows, :] = carry[1][c]
        comp_ref[3, rows, :] = carry[0]


def main_pass(velocity, before, after, table):
    comps, depth, width, length = velocity.shape
    hbm = pl.BlockSpec(memory_space=pl.ANY)
    return pl.pallas_call(
        main_kernel,
        grid=(8,),
        in_specs=[hbm, hbm, hbm, pl.BlockSpec((16, 8, 128), lambda j: (0, 0, 0))],
        out_specs=[
            pl.BlockSpec((4, width, 128), lambda j: (0, 0, j)),
            pl.BlockSpec((4, 2, 8, 8, 128), lambda j: (0, 0, 0, 0, j)),
        ],
        out_shape=[
            jax.ShapeDtypeStruct((4, width, length), F32),
            jax.ShapeDtypeStruct((4, 2, 8, 8, length), F32),
        ],
        scratch_shapes=[pltpu.VMEM((comps, depth + 4, width, length + 256), F32), pltpu.SemaphoreType.DMA((3, 8))],
        compiler_params=pltpu.CompilerParams(vmem_limit_bytes=VMEM_LIMIT),
        cost_estimate=pl.CostEstimate(flops=60000000, bytes_accessed=10000000, transcendentals=1000000),
        name="main_pass",
    )(velocity, before, after, table)


def edge_kernel(edge_ref, lo_ref, hi_ref, comp_ref, tab_ref, out_ref):
    for j in range(8):
        lanes = slice(j * 128, j * 128 + 128)
        out_ref[j] = comp_ref[:, :, lanes]
        for side, halo_ref in enumerate((lo_ref, hi_ref)):
            zeros = jnp.zeros((8, 128), F32)
            carry = (zeros + 1.0, [zeros] * 3)
            for zz in range(8):
                part, by_z, by_x, by_y = [edge_ref[e, side, zz, :, lanes] for e in range(4)]
                hz, hx, hy = [halo_ref[c, zz, :, lanes] for c in range(3)]
                total = part + by_z * hz + by_y * hy + hx * (by_x + hx)
                step, colors = lookup(QSCALE * total, tab_ref)
                carry = composite(carry, step, colors)
            trans, shades = carry
            for back in (2, 4):
                shades = [s + trans * pltpu.roll(s, 8 - back, 0) for s in shades]
                trans = trans * pltpu.roll(trans, 8 - back, 0)
            start = 14 * side
            for c in range(3):
                out_ref[j, c, start : start + 2, :] = shades[c][0:2]
            out_ref[j, 3, start : start + 2, :] = trans[0:2]


def edge_pass(edge, lo, hi, comp, table):
    width = comp.shape[1]
    return pl.pallas_call(
        edge_kernel,
        out_shape=jax.ShapeDtypeStruct((8, 4, width, 128), F32),
        compiler_params=pltpu.CompilerParams(vmem_limit_bytes=VMEM_LIMIT),
        cost_estimate=pl.CostEstimate(flops=10000000, bytes_accessed=4000000, transcendentals=300000),
        name="edge_pass",
    )(edge, lo, hi, comp, table)


def over_kernel(parts_ref, out_ref):
    shades = [parts_ref[7, c] for c in range(3)]
    trans = parts_ref[7, 3]
    for layer in range(6, -1, -1):
        front = parts_ref[layer, 3]
        shades = [parts_ref[layer, c] + front * s for c, s in enumerate(shades)]
        trans = trans * front
    for c in range(3):
        out_ref[c] = shades[c]
    out_ref[3] = trans


def over(parts):
    return pl.pallas_call(
        over_kernel,
        out_shape=jax.ShapeDtypeStruct(parts.shape[1:], F32),
        name="over",
    )(parts)


def make_table(sigma_table, color_table, depth_total):
    values = jnp.concatenate([sigma_table[None] * (-1.0 / depth_total), color_table], axis=0)
    slopes = values[:, 1:] - values[:, :-1]
    starts = values[:, :-1] - slopes * jnp.arange(15, dtype=F32)
    table = jnp.concatenate([starts, slopes], axis=0)
    table = jnp.pad(table, ((0, 0), (0, 1))).reshape(16, 8, 1)
    return jnp.broadcast_to(table, (16, 8, 128))


def local(velocity, sigma_table, color_table):
    layers, tiles = lax.axis_size("depth"), lax.axis_size("tile")
    table = make_table(sigma_table, color_table, velocity.shape[1] * layers)
    up, down, zup, zdown = pack(velocity)
    lo = lax.ppermute(up, "tile", shift_up(tiles))
    hi = lax.ppermute(down, "tile", shift_down(tiles))
    before = lax.ppermute(zup, "depth", shift_up(layers))
    after = lax.ppermute(zdown, "depth", shift_down(layers))
    comp, edge = main_pass(velocity, before, after, table)
    pieces = edge_pass(edge, lo, hi, comp, table)
    received = lax.all_to_all(pieces, "depth", split_axis=0, concat_axis=0, tiled=True)
    return over(received)


def solution(mesh):
    return jax.shard_map(
        local,
        mesh=mesh,
        in_specs=(P(None, "depth", "tile", None), P(), P()),
        out_specs=P(None, "tile", "depth"),
        check_vma=False,
    )
```

```python
import jax
import jax.numpy as jnp
from jax import lax
from jax.experimental import pallas as pl
from jax.experimental.pallas import tpu as pltpu
from jax.sharding import PartitionSpec as P

F32 = jnp.float32
VMEM_LIMIT = 40 * 1024 * 1024
VMEM_ALL = 50 * 1024 * 1024
QSCALE = -1.0 / 1152.0


def shift_up(count):
    return [(i, i + 1) for i in range(count - 1)]


def shift_down(count):
    return [(i + 1, i) for i in range(count - 1)]


def pack_kernel(v_ref, up_ref, down_ref, zup_ref, zdown_ref):
    half = pl.program_id(1)

    @pl.when(half == 0)
    def _():
        zdown_ref[...] = v_ref[:, 0, 0:2]

    @pl.when(half == 1)
    def _():
        zup_ref[...] = v_ref[:, 3, 2:4]

    row = lax.broadcasted_iota(jnp.int32, (8, 1024), 0)
    for quarter in range(4):
        for zz in range(4):
            low = v_ref[0, quarter, zz, 0:8, :]
            high = v_ref[0, quarter, zz, 8:16, :]
            up = jnp.where(row == 6, high - 8.0 * pltpu.roll(high, 7, 0), high)
            down = jnp.where(row == 0, -low, 8.0 * pltpu.roll(low, 1, 0) - low)
            up_ref[0, zz, 2 * quarter : 2 * quarter + 2, :] = up[6:8]
            down_ref[0, zz, 2 * quarter : 2 * quarter + 2, :] = down[0:2]


def pack(velocity):
    comps, depth, width, length = velocity.shape
    ends = jax.ShapeDtypeStruct((comps, 8, 8, length), F32)
    layers = jax.ShapeDtypeStruct((comps, 2, width, length), F32)
    end_block = pl.BlockSpec((1, 4, 8, length), lambda c, h: (c, h, 0, 0))
    layer_block = pl.BlockSpec((1, 2, width, length), lambda c, h: (c, 0, 0, 0))
    return pl.pallas_call(
        pack_kernel,
        grid=(comps, 2),
        in_specs=[pl.BlockSpec((1, 4, 4, width, length), lambda c, h: (c, 0, h, 0, 0))],
        out_specs=[end_block] * 2 + [layer_block] * 2,
        out_shape=[ends, ends, layers, layers],
        compiler_params=pltpu.CompilerParams(vmem_limit_bytes=VMEM_ALL),
        cost_estimate=pl.CostEstimate(flops=2000000, bytes_accessed=9000000, transcendentals=0),
        name="pack",
    )(velocity.reshape(comps, 4, 8, width, length))


def lookup(qcrit, tab_ref):
    pos = 7.5 * jnp.tanh(qcrit) + 7.5
    index = jnp.minimum(pos.astype(jnp.int32), 14)
    low, index = index < 8, index & 7
    pick = lambda k: jnp.take_along_axis(tab_ref[k], index, axis=0, mode="promise_in_bounds")
    base = [jnp.where(low, pick(2 * k), pick(2 * k + 1)) for k in range(8)]
    vals = [base[k] + base[k + 4] * pos for k in range(4)]
    return jnp.exp(vals[0]), vals[1:]


def composite(carry, step, colors):
    trans, shades = carry
    after = trans * step
    weight = trans - after
    return after, [s + weight * c for s, c in zip(shades, colors)]


def edge_masks():
    row = lax.broadcasted_iota(jnp.int32, (8, 128), 0)
    lane = lax.broadcasted_iota(jnp.int32, (8, 128), 1)
    return (row < 1, row > 6, row < 2, row > 5), (lane < 1, lane > 126, lane < 2, lane > 125)


def gradients(window, others, lefts, rights, side, masks):
    (r1, r7, r2, r6), (l1, l7, l2, l6) = masks
    dz, dx, dy = [], [], []
    for c in range(3):
        w = window[c]
        center = w[2]
        dz.append(8.0 * (w[3] - w[1]) - (w[4] - w[0]))
        above, below = (0.0, others[c]) if side == 0 else (others[c], 0.0)
        p1 = pltpu.roll(jnp.where(r1, below, center), 7, 0)
        m1 = pltpu.roll(jnp.where(r7, above, center), 1, 0)
        p2 = pltpu.roll(jnp.where(r2, below, center), 6, 0)
        m2 = pltpu.roll(jnp.where(r6, above, center), 2, 0)
        dx.append(8.0 * (p1 - m1) - (p2 - m2))
        p1 = pltpu.roll(jnp.where(l1, rights[c], center), 127, 1)
        m1 = pltpu.roll(jnp.where(l7, lefts[c], center), 1, 1)
        p2 = pltpu.roll(jnp.where(l2, rights[c], center), 126, 1)
        m2 = pltpu.roll(jnp.where(l6, lefts[c], center), 2, 1)
        dy.append(8.0 * (p1 - m1) - (p2 - m2))
    return dz, dx, dy


def invariant(dz, dx, dy):
    cross = dz[1] * dx[0] + dz[2] * dy[0] + dx[2] * dy[1]
    return dz[0] * dz[0] + dx[1] * dx[1] + dy[2] * dy[2] + 2.0 * cross


def edge_terms(total, dz, dx, dy):
    return total, 2.0 * dz[1], 2.0 * dx[1], 2.0 * dy[1]


def middle_kernel(v_hbm, tab_ref, comp_ref, edge_ref, buf, sems):
    j = pl.program_id(0)

    def copy(k):
        lanes = pl.ds(pl.multiple_of(k * 128, 128), 128)
        inner = pl.ds(pl.multiple_of((k + 1) * 128, 128), 128)
        return pltpu.make_async_copy(v_hbm.at[:, :, :, lanes], buf.at[:, :, :, inner], sems.at[k])

    @pl.when(j == 0)
    def _():
        for k in range(8):
            copy(k).start()
        zeros = jnp.zeros((3, 32, 16, 128), F32)
        buf[:, :, :, 0:128] = zeros
        buf[:, :, :, 9 * 128 : 10 * 128] = zeros
        copy(0).wait()

    @pl.when(j < 7)
    def _():
        copy(j + 1).wait()

    masks = edge_masks()
    left = pl.ds(pl.multiple_of(j * 128, 128), 128)
    mid = pl.ds(pl.multiple_of(j * 128 + 128, 128), 128)
    right = pl.ds(pl.multiple_of(j * 128 + 256, 128), 128)
    for side in range(2):
        rows = slice(8 * side, 8 * side + 8)
        others = slice(8 - 8 * side, 16 - 8 * side)
        zeros = jnp.zeros((8, 128), F32)
        carry = (zeros + 1.0, [zeros] * 3)
        lines = [[buf[c, z, rows, mid] for z in range(32)] for c in range(3)]
        for z in range(2, 30):
            quarter, zz = z // 8, z % 8
            dz, dx, dy = gradients(
                [lines[c][z - 2 : z + 3] for c in range(3)],
                [buf[c, z, others, mid] for c in range(3)],
                [buf[c, z, rows, left] for c in range(3)],
                [buf[c, z, rows, right] for c in range(3)],
                side,
                masks,
            )
            total = invariant(dz, dx, dy)
            ends = slice(6 * side, 6 * side + 2)
            for e, value in enumerate(edge_terms(total, dz, dx, dy)):
                edge_ref[e, side, zz, 2 * quarter : 2 * quarter + 2, :] = value[ends]
            step, colors = lookup(QSCALE * total, tab_ref)
            carry = composite(carry, step, colors)
        for c in range(3):
            comp_ref[c, rows, :] = carry[1][c]
        comp_ref[3, rows, :] = carry[0]


def middle_pass(velocity, table):
    comps, depth, width, length = velocity.shape
    return pl.pallas_call(
        middle_kernel,
        grid=(8,),
        in_specs=[pl.BlockSpec(memory_space=pl.ANY), pl.BlockSpec((16, 8, 128), lambda j: (0, 0, 0))],
        out_specs=[
            pl.BlockSpec((4, width, 128), lambda j: (0, 0, j)),
            pl.BlockSpec((4, 2, 8, 8, 128), lambda j: (0, 0, 0, 0, j)),
        ],
        out_shape=[
            jax.ShapeDtypeStruct((4, width, length), F32),
            jax.ShapeDtypeStruct((4, 2, 8, 8, length), F32),
        ],
        scratch_shapes=[pltpu.VMEM((comps, depth, width, length + 256), F32), pltpu.SemaphoreType.DMA((8,))],
        compiler_params=pltpu.CompilerParams(vmem_limit_bytes=VMEM_ALL),
        cost_estimate=pl.CostEstimate(flops=60000000, bytes_accessed=10000000, transcendentals=1000000),
        name="middle_pass",
    )(velocity, table)


def ends_kernel(v_hbm, zlo_ref, zhi_ref, comp_ref, tab_ref, out_ref, edge_ref, buf, sems):
    copies = [pltpu.make_async_copy(v_hbm.at[:, 28 * k : 28 * k + 4], buf.at[k], sems.at[k]) for k in range(2)]
    for copy in copies:
        copy.start()
    for copy in copies:
        copy.wait()
    masks = edge_masks()
    zeros = jnp.zeros((8, 128), F32)
    for j in range(8):
        lanes = slice(j * 128, j * 128 + 128)
        for side in range(2):
            rows = slice(8 * side, 8 * side + 8)
            others = slice(8 - 8 * side, 16 - 8 * side)
            carry = (zeros + 1.0, [zeros] * 3)
            for k in range(2):
                first = [[zlo_ref[c, i, rows, lanes] for i in range(2)] for c in range(3)] if k == 0 else [[]] * 3
                last = [[zhi_ref[c, i, rows, lanes] for i in range(2)] for c in range(3)] if k == 1 else [[]] * 3
                lines = [first[c] + [buf[k, c, i, rows, lanes] for i in range(4)] + last[c] for c in range(3)]
                for i in range(2):
                    at = i + 2 * k
                    sideways = lambda m: [
                        buf[k, c, at, rows, m * 128 : m * 128 + 128] if 0 <= m < 8 else zeros for c in range(3)
                    ]
                    dz, dx, dy = gradients(
                        [lines[c][i : i + 5] for c in range(3)],
                        [buf[k, c, at, others, lanes] for c in range(3)],
                        sideways(j - 1),
                        sideways(j + 1),
                        side,
                        masks,
                    )
                    total = invariant(dz, dx, dy)
                    ends = slice(6 * side, 6 * side + 2)
                    for e, value in enumerate(edge_terms(total, dz, dx, dy)):
                        edge_ref[e, side, i, 6 * k : 6 * k + 2, lanes] = value[ends]
                    step, colors = lookup(QSCALE * total, tab_ref)
                    carry = composite(carry, step, colors)
                if k == 0:
                    trans, shades = carry
                    shades = [s + trans * comp_ref[c, rows, lanes] for c, s in enumerate(shades)]
                    carry = (trans * comp_ref[3, rows, lanes], shades)
            for c in range(3):
                out_ref[c, rows, lanes] = carry[1][c]
            out_ref[3, rows, lanes] = carry[0]


def ends_pass(velocity, before, after, comp, table):
    comps, depth, width, length = velocity.shape
    vmem = pl.BlockSpec(memory_space=pltpu.VMEM)
    return pl.pallas_call(
        ends_kernel,
        in_specs=[pl.BlockSpec(memory_space=pl.ANY)] + [vmem] * 4,
        out_shape=[
            jax.ShapeDtypeStruct((4, width, length), F32),
            jax.ShapeDtypeStruct((4, 2, 2, 8, length), F32),
        ],
        scratch_shapes=[pltpu.VMEM((2, comps, 4, width, length), F32), pltpu.SemaphoreType.DMA((2,))],
        compiler_params=pltpu.CompilerParams(vmem_limit_bytes=VMEM_ALL),
        cost_estimate=pl.CostEstimate(flops=8000000, bytes_accessed=3000000, transcendentals=130000),
        name="ends_pass",
    )(velocity, before, after, comp, table)


def edge_kernel(edge_ref, ends_ref, lo_ref, hi_ref, comp_ref, tab_ref, out_ref):
    row = lax.broadcasted_iota(jnp.int32, (8, 128), 0)
    first, last = row < 2, row > 5
    for j in range(8):
        lanes = slice(j * 128, j * 128 + 128)
        out_ref[j] = comp_ref[:, :, lanes]
        for side, halo_ref in enumerate((lo_ref, hi_ref)):
            zeros = jnp.zeros((8, 128), F32)
            carry = (zeros + 1.0, [zeros] * 3)
            for zz in range(8):
                terms = [edge_ref[e, side, zz, :, lanes] for e in range(4)]
                if zz < 2:
                    terms = [jnp.where(first, ends_ref[e, side, zz, :, lanes], t) for e, t in enumerate(terms)]
                if zz > 5:
                    terms = [jnp.where(last, ends_ref[e, side, zz - 6, :, lanes], t) for e, t in enumerate(terms)]
                part, by_z, by_x, by_y = terms
                hz, hx, hy = [halo_ref[c, zz, :, lanes] for c in range(3)]
                total = part + by_z * hz + by_y * hy + hx * (by_x + hx)
                step, colors = lookup(QSCALE * total, tab_ref)
                carry = composite(carry, step, colors)
            trans, shades = carry
            for back in (2, 4):
                shades = [s + trans * pltpu.roll(s, 8 - back, 0) for s in shades]
                trans = trans * pltpu.roll(trans, 8 - back, 0)
            start = 14 * side
            for c in range(3):
                out_ref[j, c, start : start + 2, :] = shades[c][0:2]
            out_ref[j, 3, start : start + 2, :] = trans[0:2]


def edge_pass(edge, ends, lo, hi, comp, table):
    width = comp.shape[1]
    return pl.pallas_call(
        edge_kernel,
        out_shape=jax.ShapeDtypeStruct((8, 4, width, 128), F32),
        compiler_params=pltpu.CompilerParams(vmem_limit_bytes=VMEM_LIMIT),
        cost_estimate=pl.CostEstimate(flops=10000000, bytes_accessed=4000000, transcendentals=300000),
        name="edge_pass",
    )(edge, ends, lo, hi, comp, table)


def over(parts):
    result = parts[7]
    for layer in range(6, -1, -1):
        front = parts[layer]
        shade = front[:3] + front[3:] * result[:3]
        result = jnp.concatenate([shade, front[3:] * result[3:]], axis=0)
    return result


def make_table(sigma_table, color_table, depth_total):
    values = jnp.concatenate([sigma_table[None] * (-1.0 / depth_total), color_table], axis=0)
    slopes = values[:, 1:] - values[:, :-1]
    starts = values[:, :-1] - slopes * jnp.arange(15, dtype=F32)
    table = jnp.concatenate([starts, slopes], axis=0)
    table = jnp.pad(table, ((0, 0), (0, 1))).reshape(16, 8, 1)
    return jnp.broadcast_to(table, (16, 8, 128))


def local(velocity, sigma_table, color_table):
    layers, tiles = lax.axis_size("depth"), lax.axis_size("tile")
    table = make_table(sigma_table, color_table, velocity.shape[1] * layers)
    up, down, zup, zdown = pack(velocity)
    lo = lax.ppermute(up, "tile", shift_up(tiles))
    hi = lax.ppermute(down, "tile", shift_down(tiles))
    before = lax.ppermute(zup, "depth", shift_up(layers))
    after = lax.ppermute(zdown, "depth", shift_down(layers))
    comp, edge = middle_pass(velocity, table)
    comp, ends = ends_pass(velocity, before, after, comp, table)
    pieces = edge_pass(edge, ends, lo, hi, comp, table)
    received = lax.all_to_all(pieces, "depth", split_axis=0, concat_axis=0, tiled=True)
    return over(received)


def solution(mesh):
    return jax.shard_map(
        local,
        mesh=mesh,
        in_specs=(P(None, "depth", "tile", None), P(), P()),
        out_specs=P(None, "tile", "depth"),
        check_vma=False,
    )
```

```python
import jax
import jax.numpy as jnp
from jax import lax
from jax.experimental import pallas as pl
from jax.experimental.pallas import tpu as pltpu
from jax.sharding import PartitionSpec as P

F32 = jnp.float32
VMEM_LIMIT = 40 * 1024 * 1024
VMEM_ALL = 50 * 1024 * 1024
QSCALE = -1.0 / 1152.0


def ring(count, by):
    return [(i, (i + by) % count) for i in range(count)]


def pack_kernel(v_hbm, up_ref, down_ref, zup_ref, zdown_ref, buf, sems):
    copies = [
        [pltpu.make_async_copy(v_hbm.at[c, 8 * q : 8 * q + 8], buf.at[c, 8 * q : 8 * q + 8], sems.at[c, q]) for q in range(4)]
        for c in range(3)
    ]
    for some in copies:
        for copy in some:
            copy.start()
    tile, tiles = lax.axis_index("tile"), lax.axis_size("tile")
    layer, layers = lax.axis_index("depth"), lax.axis_size("depth")
    keep_up = jnp.where(tile == tiles - 1, 0.0, 1.0)
    keep_down = jnp.where(tile == 0, 0.0, 1.0)
    keep_zup = jnp.where(layer == layers - 1, 0.0, 1.0)
    keep_zdown = jnp.where(layer == 0, 0.0, 1.0)
    row = lax.broadcasted_iota(jnp.int32, (8, 1024), 0)
    for c in range(3):
        for quarter in range(4):
            copies[c][quarter].wait()
            for zz in range(8):
                z = quarter * 8 + zz
                low = buf[c, z, 0:8, :]
                high = buf[c, z, 8:16, :]
                up = jnp.where(row == 6, high - 8.0 * pltpu.roll(high, 7, 0), high)
                down = jnp.where(row == 0, -low, 8.0 * pltpu.roll(low, 1, 0) - low)
                up_ref[c, zz, 2 * quarter : 2 * quarter + 2, :] = keep_up * up[6:8]
                down_ref[c, zz, 2 * quarter : 2 * quarter + 2, :] = keep_down * down[0:2]
        zdown_ref[c] = keep_zdown * buf[c, 0:2]
        zup_ref[c] = keep_zup * buf[c, 30:32]


def pack(velocity):
    comps, depth, width, length = velocity.shape
    ends = jax.ShapeDtypeStruct((comps, 8, 8, length), F32)
    layers = jax.ShapeDtypeStruct((comps, 2, width, length), F32)
    return pl.pallas_call(
        pack_kernel,
        in_specs=[pl.BlockSpec(memory_space=pl.ANY)],
        out_shape=[ends, ends, layers, layers],
        scratch_shapes=[pltpu.VMEM((comps, depth, width, length), F32), pltpu.SemaphoreType.DMA((comps, 4))],
        compiler_params=pltpu.CompilerParams(vmem_limit_bytes=VMEM_ALL),
        cost_estimate=pl.CostEstimate(flops=2000000, bytes_accessed=9000000, transcendentals=0),
        name="pack",
    )(velocity)


def lookup(qcrit, tab_ref):
    pos = 7.5 * jnp.tanh(qcrit) + 7.5
    index = jnp.minimum(pos.astype(jnp.int32), 14)
    low, index = index < 8, index & 7
    pick = lambda k: jnp.take_along_axis(tab_ref[k], index, axis=0, mode="promise_in_bounds")
    base = [jnp.where(low, pick(2 * k), pick(2 * k + 1)) for k in range(8)]
    vals = [base[k] + base[k + 4] * pos for k in range(4)]
    return jnp.exp(vals[0]), vals[1:]


def composite(carry, step, colors):
    trans, shades = carry
    after = trans * step
    weight = trans - after
    return after, [s + weight * c for s, c in zip(shades, colors)]


def edge_masks():
    row = lax.broadcasted_iota(jnp.int32, (8, 128), 0)
    lane = lax.broadcasted_iota(jnp.int32, (8, 128), 1)
    return (row < 1, row > 6, row < 2, row > 5), (lane < 1, lane > 126, lane < 2, lane > 125)


def gradients(window, others, lefts, rights, side, masks):
    (r1, r7, r2, r6), (l1, l7, l2, l6) = masks
    dz, dx, dy = [], [], []
    for c in range(3):
        w = window[c]
        center = w[2]
        dz.append(8.0 * (w[3] - w[1]) - (w[4] - w[0]))
        above, below = (0.0, others[c]) if side == 0 else (others[c], 0.0)
        p1 = pltpu.roll(jnp.where(r1, below, center), 7, 0)
        m1 = pltpu.roll(jnp.where(r7, above, center), 1, 0)
        p2 = pltpu.roll(jnp.where(r2, below, center), 6, 0)
        m2 = pltpu.roll(jnp.where(r6, above, center), 2, 0)
        dx.append(8.0 * (p1 - m1) - (p2 - m2))
        p1 = pltpu.roll(jnp.where(l1, rights[c], center), 127, 1)
        m1 = pltpu.roll(jnp.where(l7, lefts[c], center), 1, 1)
        p2 = pltpu.roll(jnp.where(l2, rights[c], center), 126, 1)
        m2 = pltpu.roll(jnp.where(l6, lefts[c], center), 2, 1)
        dy.append(8.0 * (p1 - m1) - (p2 - m2))
    return dz, dx, dy


def invariant(dz, dx, dy):
    cross = dz[1] * dx[0] + dz[2] * dy[0] + dx[2] * dy[1]
    return dz[0] * dz[0] + dx[1] * dx[1] + dy[2] * dy[2] + 2.0 * cross


def edge_terms(total, dz, dx, dy):
    return total, 2.0 * dz[1], 2.0 * dx[1], 2.0 * dy[1]


def middle_kernel(v_hbm, tab_ref, comp_ref, edge_ref, buf, sems):
    j = pl.program_id(0)

    def copy(k):
        lanes = pl.ds(pl.multiple_of(k * 128, 128), 128)
        inner = pl.ds(pl.multiple_of((k + 1) * 128, 128), 128)
        return pltpu.make_async_copy(v_hbm.at[:, :, :, lanes], buf.at[:, :, :, inner], sems.at[k])

    @pl.when(j == 0)
    def _():
        for k in range(8):
            copy(k).start()
        zeros = jnp.zeros((3, 32, 16, 128), F32)
        buf[:, :, :, 0:128] = zeros
        buf[:, :, :, 9 * 128 : 10 * 128] = zeros
        copy(0).wait()

    @pl.when(j < 7)
    def _():
        copy(j + 1).wait()

    masks = edge_masks()
    left = pl.ds(pl.multiple_of(j * 128, 128), 128)
    mid = pl.ds(pl.multiple_of(j * 128 + 128, 128), 128)
    right = pl.ds(pl.multiple_of(j * 128 + 256, 128), 128)
    for side in range(2):
        rows = slice(8 * side, 8 * side + 8)
        others = slice(8 - 8 * side, 16 - 8 * side)
        zeros = jnp.zeros((8, 128), F32)
        carry = (zeros + 1.0, [zeros] * 3)
        lines = [[buf[c, z, rows, mid] for z in range(32)] for c in range(3)]
        for z in range(2, 30):
            quarter, zz = z // 8, z % 8
            dz, dx, dy = gradients(
                [lines[c][z - 2 : z + 3] for c in range(3)],
                [buf[c, z, others, mid] for c in range(3)],
                [buf[c, z, rows, left] for c in range(3)],
                [buf[c, z, rows, right] for c in range(3)],
                side,
                masks,
            )
            total = invariant(dz, dx, dy)
            ends = slice(6 * side, 6 * side + 2)
            for e, value in enumerate(edge_terms(total, dz, dx, dy)):
                edge_ref[e, side, zz, 2 * quarter : 2 * quarter + 2, :] = value[ends]
            step, colors = lookup(QSCALE * total, tab_ref)
            carry = composite(carry, step, colors)
        for c in range(3):
            comp_ref[c, rows, :] = carry[1][c]
        comp_ref[3, rows, :] = carry[0]


def middle_pass(velocity, table):
    comps, depth, width, length = velocity.shape
    return pl.pallas_call(
        middle_kernel,
        grid=(8,),
        in_specs=[pl.BlockSpec(memory_space=pl.ANY), pl.BlockSpec((16, 8, 128), lambda j: (0, 0, 0))],
        out_specs=[
            pl.BlockSpec((4, width, 128), lambda j: (0, 0, j)),
            pl.BlockSpec((4, 2, 8, 8, 128), lambda j: (0, 0, 0, 0, j)),
        ],
        out_shape=[
            jax.ShapeDtypeStruct((4, width, length), F32),
            jax.ShapeDtypeStruct((4, 2, 8, 8, length), F32),
        ],
        scratch_shapes=[pltpu.VMEM((comps, depth, width, length + 256), F32), pltpu.SemaphoreType.DMA((8,))],
        compiler_params=pltpu.CompilerParams(vmem_limit_bytes=VMEM_ALL),
        cost_estimate=pl.CostEstimate(flops=60000000, bytes_accessed=10000000, transcendentals=1000000),
        name="middle_pass",
    )(velocity, table)


def ends_kernel(v_hbm, zlo_ref, zhi_ref, comp_ref, tab_ref, out_ref, edge_ref, buf, sems):
    copies = [pltpu.make_async_copy(v_hbm.at[:, 28 * k : 28 * k + 4], buf.at[k], sems.at[k]) for k in range(2)]
    for copy in copies:
        copy.start()
    for copy in copies:
        copy.wait()
    masks = edge_masks()
    zeros = jnp.zeros((8, 128), F32)
    for j in range(8):
        lanes = slice(j * 128, j * 128 + 128)
        for side in range(2):
            rows = slice(8 * side, 8 * side + 8)
            others = slice(8 - 8 * side, 16 - 8 * side)
            carry = (zeros + 1.0, [zeros] * 3)
            for k in range(2):
                first = [[zlo_ref[c, i, rows, lanes] for i in range(2)] for c in range(3)] if k == 0 else [[]] * 3
                last = [[zhi_ref[c, i, rows, lanes] for i in range(2)] for c in range(3)] if k == 1 else [[]] * 3
                lines = [first[c] + [buf[k, c, i, rows, lanes] for i in range(4)] + last[c] for c in range(3)]
                for i in range(2):
                    at = i + 2 * k
                    sideways = lambda m: [
                        buf[k, c, at, rows, m * 128 : m * 128 + 128] if 0 <= m < 8 else zeros for c in range(3)
                    ]
                    dz, dx, dy = gradients(
                        [lines[c][i : i + 5] for c in range(3)],
                        [buf[k, c, at, others, lanes] for c in range(3)],
                        sideways(j - 1),
                        sideways(j + 1),
                        side,
                        masks,
                    )
                    total = invariant(dz, dx, dy)
                    ends = slice(6 * side, 6 * side + 2)
                    for e, value in enumerate(edge_terms(total, dz, dx, dy)):
                        edge_ref[e, side, i, 6 * k : 6 * k + 2, lanes] = value[ends]
                    step, colors = lookup(QSCALE * total, tab_ref)
                    carry = composite(carry, step, colors)
                if k == 0:
                    trans, shades = carry
                    shades = [s + trans * comp_ref[c, rows, lanes] for c, s in enumerate(shades)]
                    carry = (trans * comp_ref[3, rows, lanes], shades)
            for c in range(3):
                out_ref[c, rows, lanes] = carry[1][c]
            out_ref[3, rows, lanes] = carry[0]


def ends_pass(velocity, before, after, comp, table):
    comps, depth, width, length = velocity.shape
    vmem = pl.BlockSpec(memory_space=pltpu.VMEM)
    return pl.pallas_call(
        ends_kernel,
        in_specs=[pl.BlockSpec(memory_space=pl.ANY)] + [vmem] * 4,
        out_shape=[
            jax.ShapeDtypeStruct((4, width, length), F32),
            jax.ShapeDtypeStruct((4, 2, 2, 8, length), F32),
        ],
        scratch_shapes=[pltpu.VMEM((2, comps, 4, width, length), F32), pltpu.SemaphoreType.DMA((2,))],
        compiler_params=pltpu.CompilerParams(vmem_limit_bytes=VMEM_ALL),
        cost_estimate=pl.CostEstimate(flops=8000000, bytes_accessed=3000000, transcendentals=130000),
        name="ends_pass",
    )(velocity, before, after, comp, table)


def edge_kernel(edge_ref, ends_ref, lo_ref, hi_ref, comp_ref, tab_ref, out_ref):
    row = lax.broadcasted_iota(jnp.int32, (8, 128), 0)
    first, last = row < 2, row > 5
    for j in range(8):
        lanes = slice(j * 128, j * 128 + 128)
        out_ref[j] = comp_ref[:, :, lanes]
        for side, halo_ref in enumerate((lo_ref, hi_ref)):
            zeros = jnp.zeros((8, 128), F32)
            carry = (zeros + 1.0, [zeros] * 3)
            for zz in range(8):
                terms = [edge_ref[e, side, zz, :, lanes] for e in range(4)]
                if zz < 2:
                    terms = [jnp.where(first, ends_ref[e, side, zz, :, lanes], t) for e, t in enumerate(terms)]
                if zz > 5:
                    terms = [jnp.where(last, ends_ref[e, side, zz - 6, :, lanes], t) for e, t in enumerate(terms)]
                part, by_z, by_x, by_y = terms
                hz, hx, hy = [halo_ref[c, zz, :, lanes] for c in range(3)]
                total = part + by_z * hz + by_y * hy + hx * (by_x + hx)
                step, colors = lookup(QSCALE * total, tab_ref)
                carry = composite(carry, step, colors)
            trans, shades = carry
            for back in (2, 4):
                shades = [s + trans * pltpu.roll(s, 8 - back, 0) for s in shades]
                trans = trans * pltpu.roll(trans, 8 - back, 0)
            start = 14 * side
            for c in range(3):
                out_ref[j, c, start : start + 2, :] = shades[c][0:2]
            out_ref[j, 3, start : start + 2, :] = trans[0:2]


def edge_pass(edge, ends, lo, hi, comp, table):
    width = comp.shape[1]
    return pl.pallas_call(
        edge_kernel,
        out_shape=jax.ShapeDtypeStruct((8, 4, width, 128), F32),
        compiler_params=pltpu.CompilerParams(vmem_limit_bytes=VMEM_LIMIT),
        cost_estimate=pl.CostEstimate(flops=10000000, bytes_accessed=4000000, transcendentals=300000),
        name="edge_pass",
    )(edge, ends, lo, hi, comp, table)


def over(parts):
    result = parts[7]
    for layer in range(6, -1, -1):
        front = parts[layer]
        shade = front[:3] + front[3:] * result[:3]
        result = jnp.concatenate([shade, front[3:] * result[3:]], axis=0)
    return result


def make_table(sigma_table, color_table, depth_total):
    values = jnp.concatenate([sigma_table[None] * (-1.0 / depth_total), color_table], axis=0)
    slopes = values[:, 1:] - values[:, :-1]
    starts = values[:, :-1] - slopes * jnp.arange(15, dtype=F32)
    table = jnp.concatenate([starts, slopes], axis=0)
    table = jnp.pad(table, ((0, 0), (0, 1))).reshape(16, 8, 1)
    return jnp.broadcast_to(table, (16, 8, 128))


def local(velocity, sigma_table, color_table):
    layers, tiles = lax.axis_size("depth"), lax.axis_size("tile")
    table = make_table(sigma_table, color_table, velocity.shape[1] * layers)
    up, down, zup, zdown = pack(velocity)
    lo = lax.ppermute(up, "tile", ring(tiles, 1))
    hi = lax.ppermute(down, "tile", ring(tiles, -1))
    before = lax.ppermute(zup, "depth", ring(layers, 1))
    after = lax.ppermute(zdown, "depth", ring(layers, -1))
    comp, edge = middle_pass(velocity, table)
    comp, ends = ends_pass(velocity, before, after, comp, table)
    pieces = edge_pass(edge, ends, lo, hi, comp, table)
    received = lax.all_to_all(pieces, "depth", split_axis=0, concat_axis=0, tiled=True)
    return over(received)


def solution(mesh):
    return jax.shard_map(
        local,
        mesh=mesh,
        in_specs=(P(None, "depth", "tile", None), P(), P()),
        out_specs=P(None, "tile", "depth"),
        check_vma=False,
    )
```

```python
import jax
import jax.numpy as jnp
from jax import lax
from jax.experimental import pallas as pl
from jax.experimental.pallas import tpu as pltpu
from jax.sharding import PartitionSpec as P

F32 = jnp.float32
VMEM_LIMIT = 40 * 1024 * 1024
VMEM_ALL = 50 * 1024 * 1024
QSCALE = -1.0 / 1152.0


def ring(count, by):
    return [(i, (i + by) % count) for i in range(count)]


def pack_kernel(v_hbm, up_ref, down_ref, zup_ref, zdown_ref, buf, sems):
    copies = [
        [pltpu.make_async_copy(v_hbm.at[c, 8 * q : 8 * q + 8], buf.at[c, 8 * q : 8 * q + 8], sems.at[c, q]) for q in range(4)]
        for c in range(3)
    ]
    for some in copies:
        for copy in some:
            copy.start()
    tile, tiles = lax.axis_index("tile"), lax.axis_size("tile")
    layer, layers = lax.axis_index("depth"), lax.axis_size("depth")
    keep_up = jnp.where(tile == tiles - 1, 0.0, 1.0)
    keep_down = jnp.where(tile == 0, 0.0, 1.0)
    keep_zup = jnp.where(layer == layers - 1, 0.0, 1.0)
    keep_zdown = jnp.where(layer == 0, 0.0, 1.0)
    row = lax.broadcasted_iota(jnp.int32, (8, 1024), 0)
    for c in range(3):
        for quarter in range(4):
            copies[c][quarter].wait()
            for zz in range(8):
                z = quarter * 8 + zz
                low = buf[c, z, 0:8, :]
                high = buf[c, z, 8:16, :]
                up = jnp.where(row == 6, high - 8.0 * pltpu.roll(high, 7, 0), high)
                down = jnp.where(row == 0, -low, 8.0 * pltpu.roll(low, 1, 0) - low)
                up_ref[c, zz, 2 * quarter : 2 * quarter + 2, :] = keep_up * up[6:8]
                down_ref[c, zz, 2 * quarter : 2 * quarter + 2, :] = keep_down * down[0:2]
        zdown_ref[c] = keep_zdown * buf[c, 0:2]
        zup_ref[c] = keep_zup * buf[c, 30:32]


def pack(velocity):
    comps, depth, width, length = velocity.shape
    ends = jax.ShapeDtypeStruct((comps, 8, 8, length), F32)
    layers = jax.ShapeDtypeStruct((comps, 2, width, length), F32)
    return pl.pallas_call(
        pack_kernel,
        in_specs=[pl.BlockSpec(memory_space=pl.ANY)],
        out_shape=[ends, ends, layers, layers],
        scratch_shapes=[pltpu.VMEM((comps, depth, width, length), F32), pltpu.SemaphoreType.DMA((comps, 4))],
        compiler_params=pltpu.CompilerParams(vmem_limit_bytes=VMEM_ALL),
        cost_estimate=pl.CostEstimate(flops=2000000, bytes_accessed=9000000, transcendentals=0),
        name="pack",
    )(velocity)


def lookup(qcrit, tab_ref):
    pos = 7.5 * jnp.tanh(qcrit) + 7.5
    index = jnp.minimum(pos.astype(jnp.int32), 14)
    low, index = index < 8, index & 7
    pick = lambda k: jnp.take_along_axis(tab_ref[k], index, axis=0, mode="promise_in_bounds")
    base = [jnp.where(low, pick(2 * k), pick(2 * k + 1)) for k in range(8)]
    vals = [base[k] + base[k + 4] * pos for k in range(4)]
    return jnp.exp(vals[0]), vals[1:]


def composite(carry, step, colors):
    trans, shades = carry
    after = trans * step
    weight = trans - after
    return after, [s + weight * c for s, c in zip(shades, colors)]


def edge_masks():
    row = lax.broadcasted_iota(jnp.int32, (8, 128), 0)
    lane = lax.broadcasted_iota(jnp.int32, (8, 128), 1)
    return (row < 1, row > 6, row < 2, row > 5), (lane < 1, lane > 126, lane < 2, lane > 125)


def gradients(window, others, lefts, rights, side, masks):
    (r1, r7, r2, r6), (l1, l7, l2, l6) = masks
    dz, dx, dy = [], [], []
    for c in range(3):
        w = window[c]
        center = w[2]
        dz.append(8.0 * (w[3] - w[1]) - (w[4] - w[0]))
        above, below = (0.0, others[c]) if side == 0 else (others[c], 0.0)
        p1 = pltpu.roll(jnp.where(r1, below, center), 7, 0)
        m1 = pltpu.roll(jnp.where(r7, above, center), 1, 0)
        p2 = pltpu.roll(jnp.where(r2, below, center), 6, 0)
        m2 = pltpu.roll(jnp.where(r6, above, center), 2, 0)
        dx.append(8.0 * (p1 - m1) - (p2 - m2))
        p1 = pltpu.roll(jnp.where(l1, rights[c], center), 127, 1)
        m1 = pltpu.roll(jnp.where(l7, lefts[c], center), 1, 1)
        p2 = pltpu.roll(jnp.where(l2, rights[c], center), 126, 1)
        m2 = pltpu.roll(jnp.where(l6, lefts[c], center), 2, 1)
        dy.append(8.0 * (p1 - m1) - (p2 - m2))
    return dz, dx, dy


def invariant(dz, dx, dy):
    cross = dz[1] * dx[0] + dz[2] * dy[0] + dx[2] * dy[1]
    return dz[0] * dz[0] + dx[1] * dx[1] + dy[2] * dy[2] + 2.0 * cross


def edge_terms(total, dz, dx, dy):
    return total, 2.0 * dz[1], 2.0 * dx[1], 2.0 * dy[1]


def middle_kernel(v_hbm, tab_ref, comp_ref, edge_ref, buf, sems):
    j = pl.program_id(0)

    def copy(k):
        lanes = pl.ds(pl.multiple_of(k * 128, 128), 128)
        inner = pl.ds(pl.multiple_of((k + 1) * 128, 128), 128)
        return pltpu.make_async_copy(v_hbm.at[:, :, :, lanes], buf.at[:, :, :, inner], sems.at[k])

    @pl.when(j == 0)
    def _():
        for k in range(8):
            copy(k).start()
        zeros = jnp.zeros((3, 32, 16, 128), F32)
        buf[:, :, :, 0:128] = zeros
        buf[:, :, :, 9 * 128 : 10 * 128] = zeros
        copy(0).wait()

    @pl.when(j < 7)
    def _():
        copy(j + 1).wait()

    masks = edge_masks()
    left = pl.ds(pl.multiple_of(j * 128, 128), 128)
    mid = pl.ds(pl.multiple_of(j * 128 + 128, 128), 128)
    right = pl.ds(pl.multiple_of(j * 128 + 256, 128), 128)
    for side in range(2):
        rows = slice(8 * side, 8 * side + 8)
        others = slice(8 - 8 * side, 16 - 8 * side)
        zeros = jnp.zeros((8, 128), F32)
        carry = (zeros + 1.0, [zeros] * 3)
        lines = [[buf[c, z, rows, mid] for z in range(32)] for c in range(3)]
        for z in range(2, 30):
            quarter, zz = z // 8, z % 8
            dz, dx, dy = gradients(
                [lines[c][z - 2 : z + 3] for c in range(3)],
                [buf[c, z, others, mid] for c in range(3)],
                [buf[c, z, rows, left] for c in range(3)],
                [buf[c, z, rows, right] for c in range(3)],
                side,
                masks,
            )
            total = invariant(dz, dx, dy)
            ends = slice(6 * side, 6 * side + 2)
            for e, value in enumerate(edge_terms(total, dz, dx, dy)):
                edge_ref[e, side, zz, 2 * quarter : 2 * quarter + 2, :] = value[ends]
            step, colors = lookup(QSCALE * total, tab_ref)
            carry = composite(carry, step, colors)
        for c in range(3):
            comp_ref[c, rows, :] = carry[1][c]
        comp_ref[3, rows, :] = carry[0]


def middle_pass(velocity, table):
    comps, depth, width, length = velocity.shape
    return pl.pallas_call(
        middle_kernel,
        grid=(8,),
        in_specs=[pl.BlockSpec(memory_space=pl.ANY), pl.BlockSpec((16, 8, 128), lambda j: (0, 0, 0))],
        out_specs=[
            pl.BlockSpec((4, width, 128), lambda j: (0, 0, j)),
            pl.BlockSpec((4, 2, 8, 8, 128), lambda j: (0, 0, 0, 0, j)),
        ],
        out_shape=[
            jax.ShapeDtypeStruct((4, width, length), F32),
            jax.ShapeDtypeStruct((4, 2, 8, 8, length), F32),
        ],
        scratch_shapes=[pltpu.VMEM((comps, depth, width, length + 256), F32), pltpu.SemaphoreType.DMA((8,))],
        compiler_params=pltpu.CompilerParams(vmem_limit_bytes=VMEM_ALL),
        cost_estimate=pl.CostEstimate(flops=60000000, bytes_accessed=10000000, transcendentals=1000000),
        name="middle_pass",
    )(velocity, table)


def ends_kernel(v_hbm, zlo_ref, zhi_ref, comp_ref, tab_ref, out_ref, edge_ref, buf, sems):
    copies = [pltpu.make_async_copy(v_hbm.at[:, 28 * k : 28 * k + 4], buf.at[k], sems.at[k]) for k in range(2)]
    for copy in copies:
        copy.start()
    for copy in copies:
        copy.wait()
    masks = edge_masks()
    zeros = jnp.zeros((8, 128), F32)
    for j in range(8):
        lanes = slice(j * 128, j * 128 + 128)
        for side in range(2):
            rows = slice(8 * side, 8 * side + 8)
            others = slice(8 - 8 * side, 16 - 8 * side)
            carry = (zeros + 1.0, [zeros] * 3)
            for k in range(2):
                first = [[zlo_ref[c, i, rows, lanes] for i in range(2)] for c in range(3)] if k == 0 else [[]] * 3
                last = [[zhi_ref[c, i, rows, lanes] for i in range(2)] for c in range(3)] if k == 1 else [[]] * 3
                lines = [first[c] + [buf[k, c, i, rows, lanes] for i in range(4)] + last[c] for c in range(3)]
                for i in range(2):
                    at = i + 2 * k
                    sideways = lambda m: [
                        buf[k, c, at, rows, m * 128 : m * 128 + 128] if 0 <= m < 8 else zeros for c in range(3)
                    ]
                    dz, dx, dy = gradients(
                        [lines[c][i : i + 5] for c in range(3)],
                        [buf[k, c, at, others, lanes] for c in range(3)],
                        sideways(j - 1),
                        sideways(j + 1),
                        side,
                        masks,
                    )
                    total = invariant(dz, dx, dy)
                    ends = slice(6 * side, 6 * side + 2)
                    for e, value in enumerate(edge_terms(total, dz, dx, dy)):
                        edge_ref[e, side, i, 6 * k : 6 * k + 2, lanes] = value[ends]
                    step, colors = lookup(QSCALE * total, tab_ref)
                    carry = composite(carry, step, colors)
                if k == 0:
                    trans, shades = carry
                    shades = [s + trans * comp_ref[c, rows, lanes] for c, s in enumerate(shades)]
                    carry = (trans * comp_ref[3, rows, lanes], shades)
            for c in range(3):
                out_ref[c, rows, lanes] = carry[1][c]
            out_ref[3, rows, lanes] = carry[0]


def ends_pass(velocity, before, after, comp, table):
    comps, depth, width, length = velocity.shape
    vmem = pl.BlockSpec(memory_space=pltpu.VMEM)
    return pl.pallas_call(
        ends_kernel,
        in_specs=[pl.BlockSpec(memory_space=pl.ANY)] + [vmem] * 4,
        out_shape=[
            jax.ShapeDtypeStruct((4, width, length), F32),
            jax.ShapeDtypeStruct((4, 2, 2, 8, length), F32),
        ],
        scratch_shapes=[pltpu.VMEM((2, comps, 4, width, length), F32), pltpu.SemaphoreType.DMA((2,))],
        compiler_params=pltpu.CompilerParams(vmem_limit_bytes=VMEM_ALL),
        cost_estimate=pl.CostEstimate(flops=8000000, bytes_accessed=3000000, transcendentals=130000),
        name="ends_pass",
    )(velocity, before, after, comp, table)


def edge_kernel(edge_ref, ends_ref, lo_ref, hi_ref, comp_ref, tab_ref, mine_ref, other_ref):
    row = lax.broadcasted_iota(jnp.int32, (8, 128), 0)
    first, last = row < 2, row > 5
    core = lax.rem(lax.axis_index("depth"), 2)
    for slot, out_ref in enumerate((mine_ref, other_ref)):
        for k in range(4):
            piece = 2 * k + lax.rem(core + slot, 2)
            lanes = pl.ds(pl.multiple_of(piece * 128, 128), 128)
            out_ref[k] = comp_ref[:, :, lanes]
            for side, halo_ref in enumerate((lo_ref, hi_ref)):
                zeros = jnp.zeros((8, 128), F32)
                carry = (zeros + 1.0, [zeros] * 3)
                for zz in range(8):
                    terms = [edge_ref[e, side, zz, :, lanes] for e in range(4)]
                    if zz < 2:
                        terms = [jnp.where(first, ends_ref[e, side, zz, :, lanes], t) for e, t in enumerate(terms)]
                    if zz > 5:
                        terms = [jnp.where(last, ends_ref[e, side, zz - 6, :, lanes], t) for e, t in enumerate(terms)]
                    part, by_z, by_x, by_y = terms
                    hz, hx, hy = [halo_ref[c, zz, :, lanes] for c in range(3)]
                    total = part + by_z * hz + by_y * hy + hx * (by_x + hx)
                    step, colors = lookup(QSCALE * total, tab_ref)
                    carry = composite(carry, step, colors)
                trans, shades = carry
                for back in (2, 4):
                    shades = [s + trans * pltpu.roll(s, 8 - back, 0) for s in shades]
                    trans = trans * pltpu.roll(trans, 8 - back, 0)
                start = 14 * side
                for c in range(3):
                    out_ref[k, c, start : start + 2, :] = shades[c][0:2]
                out_ref[k, 3, start : start + 2, :] = trans[0:2]


def edge_pass(edge, ends, lo, hi, comp, table):
    pieces = jax.ShapeDtypeStruct((4, 4, comp.shape[1], 128), F32)
    return pl.pallas_call(
        edge_kernel,
        out_shape=[pieces, pieces],
        compiler_params=pltpu.CompilerParams(vmem_limit_bytes=VMEM_LIMIT),
        cost_estimate=pl.CostEstimate(flops=10000000, bytes_accessed=4000000, transcendentals=300000),
        name="edge_pass",
    )(edge, ends, lo, hi, comp, table)


def over(front, back):
    shade = front[..., :3, :, :] + front[..., 3:, :, :] * back[..., :3, :, :]
    return jnp.concatenate([shade, front[..., 3:, :, :] * back[..., 3:, :, :]], axis=-3)


def gather_over(mine, other):
    place = lax.axis_index("depth")
    core, chip = lax.rem(place, 2), lax.div(place, 2)
    got = lax.ppermute(other, "depth", [(i, i ^ 1) for i in range(8)])
    near = core == 0
    pair = over(jnp.where(near, mine, got), jnp.where(near, got, mine))
    parts = [lax.dynamic_index_in_dim(pair, chip, 0, keepdims=False)]
    for k in range(1, 4):
        piece = lax.dynamic_index_in_dim(pair, lax.rem(chip + k, 4), 0, keepdims=False)
        parts.append(lax.ppermute(piece, "depth", ring(8, 2 * k)))
    parts = jnp.stack(parts)
    result = lax.dynamic_index_in_dim(parts, lax.rem(chip + 1, 4), 0, keepdims=False)
    for source in (2, 1, 0):
        result = over(lax.dynamic_index_in_dim(parts, lax.rem(chip + 4 - source, 4), 0, keepdims=False), result)
    return result


def make_table(sigma_table, color_table, depth_total):
    values = jnp.concatenate([sigma_table[None] * (-1.0 / depth_total), color_table], axis=0)
    slopes = values[:, 1:] - values[:, :-1]
    starts = values[:, :-1] - slopes * jnp.arange(15, dtype=F32)
    table = jnp.concatenate([starts, slopes], axis=0)
    table = jnp.pad(table, ((0, 0), (0, 1))).reshape(16, 8, 1)
    return jnp.broadcast_to(table, (16, 8, 128))


def local(velocity, sigma_table, color_table):
    layers, tiles = lax.axis_size("depth"), lax.axis_size("tile")
    table = make_table(sigma_table, color_table, velocity.shape[1] * layers)
    up, down, zup, zdown = pack(velocity)
    lo = lax.ppermute(up, "tile", ring(tiles, 1))
    hi = lax.ppermute(down, "tile", ring(tiles, -1))
    before = lax.ppermute(zup, "depth", ring(layers, 1))
    after = lax.ppermute(zdown, "depth", ring(layers, -1))
    comp, edge = middle_pass(velocity, table)
    comp, ends = ends_pass(velocity, before, after, comp, table)
    mine, other = edge_pass(edge, ends, lo, hi, comp, table)
    return gather_over(mine, other)


def solution(mesh):
    return jax.shard_map(
        local,
        mesh=mesh,
        in_specs=(P(None, "depth", "tile", None), P(), P()),
        out_specs=P(None, "tile", "depth"),
        check_vma=False,
    )
```

```python
import jax
import jax.numpy as jnp
from jax import lax
from jax.experimental import pallas as pl
from jax.experimental.pallas import tpu as pltpu
from jax.sharding import PartitionSpec as P

F32 = jnp.float32
VMEM_LIMIT = 20 * 1024 * 1024
VMEM_ALL = 44 * 1024 * 1024
QSCALE = -1.0 / 1152.0


def ring(count, by):
    return [(i, (i + by) % count) for i in range(count)]


def pack_kernel(v_hbm, held_ref, up_ref, down_ref, zup_ref, zdown_ref, sems):
    length = v_hbm.shape[3]
    copies = [
        [
            pltpu.make_async_copy(
                v_hbm.at[c, 8 * q : 8 * q + 8], held_ref.at[c, 8 * q : 8 * q + 8, :, 128 : 128 + length], sems.at[c, q]
            )
            for q in range(4)
        ]
        for c in range(3)
    ]
    for some in copies:
        for copy in some:
            copy.start()
    zeros = jnp.zeros(held_ref.shape[:3] + (128,), F32)
    held_ref[:, :, :, 0:128] = zeros
    held_ref[:, :, :, 128 + length :] = zeros
    inner = slice(128, 128 + length)
    tile, tiles = lax.axis_index("tile"), lax.axis_size("tile")
    layer, layers = lax.axis_index("depth"), lax.axis_size("depth")
    keep_up = jnp.where(tile == tiles - 1, 0.0, 1.0)
    keep_down = jnp.where(tile == 0, 0.0, 1.0)
    keep_zup = jnp.where(layer == layers - 1, 0.0, 1.0)
    keep_zdown = jnp.where(layer == 0, 0.0, 1.0)
    row = lax.broadcasted_iota(jnp.int32, (8, 1024), 0)
    for c in range(3):
        for quarter in range(4):
            copies[c][quarter].wait()
            for zz in range(8):
                z = quarter * 8 + zz
                low = held_ref[c, z, 0:8, inner]
                high = held_ref[c, z, 8:16, inner]
                up = jnp.where(row == 6, high - 8.0 * pltpu.roll(high, 7, 0), high)
                down = jnp.where(row == 0, -low, 8.0 * pltpu.roll(low, 1, 0) - low)
                up_ref[c, zz, 2 * quarter : 2 * quarter + 2, :] = keep_up * up[6:8]
                down_ref[c, zz, 2 * quarter : 2 * quarter + 2, :] = keep_down * down[0:2]
        zdown_ref[c] = keep_zdown * held_ref[c, 0:2, :, inner]
        zup_ref[c] = keep_zup * held_ref[c, 30:32, :, inner]


def pack(velocity):
    comps, depth, width, length = velocity.shape
    ends = jax.ShapeDtypeStruct((comps, 8, 8, length), F32)
    layers = jax.ShapeDtypeStruct((comps, 2, width, length), F32)
    return pl.pallas_call(
        pack_kernel,
        in_specs=[pl.BlockSpec(memory_space=pl.ANY)],
        out_shape=[pltpu.VMEM((comps, depth, width, length + 256), F32), ends, ends, layers, layers],
        scratch_shapes=[pltpu.SemaphoreType.DMA((comps, 4))],
        compiler_params=pltpu.CompilerParams(vmem_limit_bytes=VMEM_ALL),
        cost_estimate=pl.CostEstimate(flops=2000000, bytes_accessed=9000000, transcendentals=0),
        name="pack",
    )(velocity)


def lookup(qcrit, tab_ref):
    pos = 7.5 * jnp.tanh(qcrit) + 7.5
    index = jnp.minimum(pos.astype(jnp.int32), 14)
    low, index = index < 8, index & 7
    pick = lambda k: jnp.take_along_axis(tab_ref[k], index, axis=0, mode="promise_in_bounds")
    base = [jnp.where(low, pick(2 * k), pick(2 * k + 1)) for k in range(8)]
    vals = [base[k] + base[k + 4] * pos for k in range(4)]
    return jnp.exp(vals[0]), vals[1:]


def composite(carry, step, colors):
    trans, shades = carry
    after = trans * step
    weight = trans - after
    return after, [s + weight * c for s, c in zip(shades, colors)]


def edge_masks():
    row = lax.broadcasted_iota(jnp.int32, (8, 128), 0)
    lane = lax.broadcasted_iota(jnp.int32, (8, 128), 1)
    return (row < 1, row > 6, row < 2, row > 5), (lane < 1, lane > 126, lane < 2, lane > 125)


def gradients(window, others, lefts, rights, side, masks):
    (r1, r7, r2, r6), (l1, l7, l2, l6) = masks
    dz, dx, dy = [], [], []
    for c in range(3):
        w = window[c]
        center = w[2]
        dz.append(8.0 * (w[3] - w[1]) - (w[4] - w[0]))
        above, below = (0.0, others[c]) if side == 0 else (others[c], 0.0)
        p1 = pltpu.roll(jnp.where(r1, below, center), 7, 0)
        m1 = pltpu.roll(jnp.where(r7, above, center), 1, 0)
        p2 = pltpu.roll(jnp.where(r2, below, center), 6, 0)
        m2 = pltpu.roll(jnp.where(r6, above, center), 2, 0)
        dx.append(8.0 * (p1 - m1) - (p2 - m2))
        p1 = pltpu.roll(jnp.where(l1, rights[c], center), 127, 1)
        m1 = pltpu.roll(jnp.where(l7, lefts[c], center), 1, 1)
        p2 = pltpu.roll(jnp.where(l2, rights[c], center), 126, 1)
        m2 = pltpu.roll(jnp.where(l6, lefts[c], center), 2, 1)
        dy.append(8.0 * (p1 - m1) - (p2 - m2))
    return dz, dx, dy


def invariant(dz, dx, dy):
    cross = dz[1] * dx[0] + dz[2] * dy[0] + dx[2] * dy[1]
    return dz[0] * dz[0] + dx[1] * dx[1] + dy[2] * dy[2] + 2.0 * cross


def edge_terms(total, dz, dx, dy):
    return total, 2.0 * dz[1], 2.0 * dx[1], 2.0 * dy[1]


def middle_kernel(held_ref, tab_ref, comp_ref, edge_ref):
    masks = edge_masks()

    @pl.loop(0, 8)
    def _(j):
        left = pl.ds(pl.multiple_of(j * 128, 128), 128)
        mid = pl.ds(pl.multiple_of(j * 128 + 128, 128), 128)
        right = pl.ds(pl.multiple_of(j * 128 + 256, 128), 128)
        for side in range(2):
            rows = slice(8 * side, 8 * side + 8)
            others = slice(8 - 8 * side, 16 - 8 * side)
            zeros = jnp.zeros((8, 128), F32)
            carry = (zeros + 1.0, [zeros] * 3)
            lines = [[held_ref[c, z, rows, mid] for z in range(32)] for c in range(3)]
            for z in range(2, 30):
                quarter, zz = z // 8, z % 8
                dz, dx, dy = gradients(
                    [lines[c][z - 2 : z + 3] for c in range(3)],
                    [held_ref[c, z, others, mid] for c in range(3)],
                    [held_ref[c, z, rows, left] for c in range(3)],
                    [held_ref[c, z, rows, right] for c in range(3)],
                    side,
                    masks,
                )
                total = invariant(dz, dx, dy)
                ends = slice(6 * side, 6 * side + 2)
                for e, value in enumerate(edge_terms(total, dz, dx, dy)):
                    edge_ref[e, side, zz, 2 * quarter : 2 * quarter + 2, left] = value[ends]
                step, colors = lookup(QSCALE * total, tab_ref)
                carry = composite(carry, step, colors)
            for c in range(3):
                comp_ref[c, rows, left] = carry[1][c]
            comp_ref[3, rows, left] = carry[0]


def middle_pass(held, table):
    comps, depth, width, length = held.shape
    length -= 256
    return pl.pallas_call(
        middle_kernel,
        out_shape=[
            jax.ShapeDtypeStruct((4, width, length), F32),
            jax.ShapeDtypeStruct((4, 2, 8, 8, length), F32),
        ],
        compiler_params=pltpu.CompilerParams(vmem_limit_bytes=VMEM_LIMIT),
        cost_estimate=pl.CostEstimate(flops=60000000, bytes_accessed=10000000, transcendentals=1000000),
        name="middle_pass",
    )(held, table)


def ends_kernel(held_ref, zlo_ref, zhi_ref, comp_ref, tab_ref, out_ref, edge_ref):
    masks = edge_masks()
    zeros = jnp.zeros((8, 128), F32)
    for j in range(8):
        lanes = slice(j * 128, j * 128 + 128)
        left, mid, right = [slice(j * 128 + m, j * 128 + m + 128) for m in (0, 128, 256)]
        for side in range(2):
            rows = slice(8 * side, 8 * side + 8)
            others = slice(8 - 8 * side, 16 - 8 * side)
            carry = (zeros + 1.0, [zeros] * 3)
            for k in range(2):
                first = [[zlo_ref[c, i, rows, lanes] for i in range(2)] for c in range(3)] if k == 0 else [[]] * 3
                last = [[zhi_ref[c, i, rows, lanes] for i in range(2)] for c in range(3)] if k == 1 else [[]] * 3
                lines = [first[c] + [held_ref[c, 28 * k + i, rows, mid] for i in range(4)] + last[c] for c in range(3)]
                for i in range(2):
                    at = 30 * k + i
                    dz, dx, dy = gradients(
                        [lines[c][i : i + 5] for c in range(3)],
                        [held_ref[c, at, others, mid] for c in range(3)],
                        [held_ref[c, at, rows, left] for c in range(3)],
                        [held_ref[c, at, rows, right] for c in range(3)],
                        side,
                        masks,
                    )
                    total = invariant(dz, dx, dy)
                    ends = slice(6 * side, 6 * side + 2)
                    for e, value in enumerate(edge_terms(total, dz, dx, dy)):
                        edge_ref[e, side, i, 6 * k : 6 * k + 2, lanes] = value[ends]
                    step, colors = lookup(QSCALE * total, tab_ref)
                    carry = composite(carry, step, colors)
                if k == 0:
                    trans, shades = carry
                    shades = [s + trans * comp_ref[c, rows, lanes] for c, s in enumerate(shades)]
                    carry = (trans * comp_ref[3, rows, lanes], shades)
            for c in range(3):
                out_ref[c, rows, lanes] = carry[1][c]
            out_ref[3, rows, lanes] = carry[0]


def ends_pass(held, before, after, comp, table):
    width, length = comp.shape[1:]
    return pl.pallas_call(
        ends_kernel,
        out_shape=[
            jax.ShapeDtypeStruct((4, width, length), F32),
            jax.ShapeDtypeStruct((4, 2, 2, 8, length), F32),
        ],
        compiler_params=pltpu.CompilerParams(vmem_limit_bytes=VMEM_LIMIT),
        cost_estimate=pl.CostEstimate(flops=8000000, bytes_accessed=3000000, transcendentals=130000),
        name="ends_pass",
    )(held, before, after, comp, table)


def edge_kernel(edge_ref, ends_ref, lo_ref, hi_ref, comp_ref, tab_ref, mine_ref, other_ref):
    row = lax.broadcasted_iota(jnp.int32, (8, 128), 0)
    first, last = row < 2, row > 5
    core = lax.rem(lax.axis_index("depth"), 2)
    for slot, out_ref in enumerate((mine_ref, other_ref)):
        for k in range(4):
            piece = 2 * k + lax.rem(core + slot, 2)
            lanes = pl.ds(pl.multiple_of(piece * 128, 128), 128)
            out_ref[k] = comp_ref[:, :, lanes]
            for side, halo_ref in enumerate((lo_ref, hi_ref)):
                zeros = jnp.zeros((8, 128), F32)
                carry = (zeros + 1.0, [zeros] * 3)
                for zz in range(8):
                    terms = [edge_ref[e, side, zz, :, lanes] for e in range(4)]
                    if zz < 2:
                        terms = [jnp.where(first, ends_ref[e, side, zz, :, lanes], t) for e, t in enumerate(terms)]
                    if zz > 5:
                        terms = [jnp.where(last, ends_ref[e, side, zz - 6, :, lanes], t) for e, t in enumerate(terms)]
                    part, by_z, by_x, by_y = terms
                    hz, hx, hy = [halo_ref[c, zz, :, lanes] for c in range(3)]
                    total = part + by_z * hz + by_y * hy + hx * (by_x + hx)
                    step, colors = lookup(QSCALE * total, tab_ref)
                    carry = composite(carry, step, colors)
                trans, shades = carry
                for back in (2, 4):
                    shades = [s + trans * pltpu.roll(s, 8 - back, 0) for s in shades]
                    trans = trans * pltpu.roll(trans, 8 - back, 0)
                start = 14 * side
                for c in range(3):
                    out_ref[k, c, start : start + 2, :] = shades[c][0:2]
                out_ref[k, 3, start : start + 2, :] = trans[0:2]


def edge_pass(edge, ends, lo, hi, comp, table):
    pieces = jax.ShapeDtypeStruct((4, 4, comp.shape[1], 128), F32)
    return pl.pallas_call(
        edge_kernel,
        out_shape=[pieces, pieces],
        compiler_params=pltpu.CompilerParams(vmem_limit_bytes=VMEM_LIMIT),
        cost_estimate=pl.CostEstimate(flops=10000000, bytes_accessed=4000000, transcendentals=300000),
        name="edge_pass",
    )(edge, ends, lo, hi, comp, table)


def over(front, back):
    shade = front[..., :3, :, :] + front[..., 3:, :, :] * back[..., :3, :, :]
    return jnp.concatenate([shade, front[..., 3:, :, :] * back[..., 3:, :, :]], axis=-3)


def gather_over(mine, other):
    place = lax.axis_index("depth")
    core, chip = lax.rem(place, 2), lax.div(place, 2)
    got = lax.ppermute(other, "depth", [(i, i ^ 1) for i in range(8)])
    near = core == 0
    pair = over(jnp.where(near, mine, got), jnp.where(near, got, mine))
    parts = [lax.dynamic_index_in_dim(pair, chip, 0, keepdims=False)]
    for k in range(1, 4):
        piece = lax.dynamic_index_in_dim(pair, lax.rem(chip + k, 4), 0, keepdims=False)
        parts.append(lax.ppermute(piece, "depth", ring(8, 2 * k)))
    parts = jnp.stack(parts)
    result = lax.dynamic_index_in_dim(parts, lax.rem(chip + 1, 4), 0, keepdims=False)
    for source in (2, 1, 0):
        result = over(lax.dynamic_index_in_dim(parts, lax.rem(chip + 4 - source, 4), 0, keepdims=False), result)
    return result


def make_table(sigma_table, color_table, depth_total):
    values = jnp.concatenate([sigma_table[None] * (-1.0 / depth_total), color_table], axis=0)
    slopes = values[:, 1:] - values[:, :-1]
    starts = values[:, :-1] - slopes * jnp.arange(15, dtype=F32)
    table = jnp.concatenate([starts, slopes], axis=0)
    table = jnp.pad(table, ((0, 0), (0, 1))).reshape(16, 8, 1)
    return jnp.broadcast_to(table, (16, 8, 128))


def local(velocity, sigma_table, color_table):
    layers, tiles = lax.axis_size("depth"), lax.axis_size("tile")
    table = make_table(sigma_table, color_table, velocity.shape[1] * layers)
    held, up, down, zup, zdown = pack(velocity)
    lo = lax.ppermute(up, "tile", ring(tiles, 1))
    hi = lax.ppermute(down, "tile", ring(tiles, -1))
    before = lax.ppermute(zup, "depth", ring(layers, 1))
    after = lax.ppermute(zdown, "depth", ring(layers, -1))
    comp, edge = middle_pass(held, table)
    comp, ends = ends_pass(held, before, after, comp, table)
    mine, other = edge_pass(edge, ends, lo, hi, comp, table)
    return gather_over(mine, other)


def solution(mesh):
    return jax.shard_map(
        local,
        mesh=mesh,
        in_specs=(P(None, "depth", "tile", None), P(), P()),
        out_specs=P(None, "tile", "depth"),
        check_vma=False,
    )
```

```python
import jax
import jax.numpy as jnp
from jax import lax
from jax.experimental import pallas as pl
from jax.experimental.pallas import tpu as pltpu
from jax.sharding import PartitionSpec as P

F32 = jnp.float32
VMEM_LIMIT = 40 * 1024 * 1024
VMEM_ALL = 50 * 1024 * 1024
QSCALE = -1.0 / 1152.0


def ring(count, by):
    return [(i, (i + by) % count) for i in range(count)]


def pack_kernel(v_hbm, up_ref, down_ref, zup_ref, zdown_ref, buf, sems):
    copies = [
        [pltpu.make_async_copy(v_hbm.at[c, 8 * q : 8 * q + 8], buf.at[c, 8 * q : 8 * q + 8], sems.at[c, q]) for q in range(4)]
        for c in range(3)
    ]
    for some in copies:
        for copy in some:
            copy.start()
    tile, tiles = lax.axis_index("tile"), lax.axis_size("tile")
    layer, layers = lax.axis_index("depth"), lax.axis_size("depth")
    keep_up = jnp.where(tile == tiles - 1, 0.0, 1.0)
    keep_down = jnp.where(tile == 0, 0.0, 1.0)
    keep_zup = jnp.where(layer == layers - 1, 0.0, 1.0)
    keep_zdown = jnp.where(layer == 0, 0.0, 1.0)
    row = lax.broadcasted_iota(jnp.int32, (8, 1024), 0)
    for c in range(3):
        for quarter in range(4):
            copies[c][quarter].wait()
            for zz in range(8):
                z = quarter * 8 + zz
                low = buf[c, z, 0:8, :]
                high = buf[c, z, 8:16, :]
                up = jnp.where(row == 6, high - 8.0 * pltpu.roll(high, 7, 0), high)
                down = jnp.where(row == 0, -low, 8.0 * pltpu.roll(low, 1, 0) - low)
                up_ref[c, zz, 2 * quarter : 2 * quarter + 2, :] = keep_up * up[6:8]
                down_ref[c, zz, 2 * quarter : 2 * quarter + 2, :] = keep_down * down[0:2]
        zdown_ref[c] = keep_zdown * buf[c, 0:2]
        zup_ref[c] = keep_zup * buf[c, 30:32]


def pack(velocity):
    comps, depth, width, length = velocity.shape
    ends = jax.ShapeDtypeStruct((comps, 8, 8, length), F32)
    layers = jax.ShapeDtypeStruct((comps, 2, width, length), F32)
    return pl.pallas_call(
        pack_kernel,
        in_specs=[pl.BlockSpec(memory_space=pl.ANY)],
        out_shape=[ends, ends, layers, layers],
        scratch_shapes=[pltpu.VMEM((comps, depth, width, length), F32), pltpu.SemaphoreType.DMA((comps, 4))],
        compiler_params=pltpu.CompilerParams(vmem_limit_bytes=VMEM_ALL),
        cost_estimate=pl.CostEstimate(flops=2000000, bytes_accessed=9000000, transcendentals=0),
        name="pack",
    )(velocity)


def lookup(qcrit, tab_ref):
    pos = 7.5 * jnp.tanh(qcrit) + 7.5
    index = jnp.minimum(pos.astype(jnp.int32), 14)
    low, index = index < 8, index & 7
    pick = lambda k: jnp.take_along_axis(tab_ref[k], index, axis=0, mode="promise_in_bounds")
    base = [jnp.where(low, pick(2 * k), pick(2 * k + 1)) for k in range(8)]
    vals = [base[k] + base[k + 4] * pos for k in range(4)]
    return jnp.exp(vals[0]), vals[1:]


def composite(carry, step, colors):
    trans, shades = carry
    after = trans * step
    weight = trans - after
    return after, [s + weight * c for s, c in zip(shades, colors)]


def edge_masks():
    row = lax.broadcasted_iota(jnp.int32, (8, 128), 0)
    lane = lax.broadcasted_iota(jnp.int32, (8, 128), 1)
    return (row < 1, row > 6, row < 2, row > 5), (lane < 1, lane > 126, lane < 2, lane > 125)


def gradients(window, others, lefts, rights, side, masks):
    (r1, r7, r2, r6), (l1, l7, l2, l6) = masks
    dz, dx, dy = [], [], []
    for c in range(3):
        w = window[c]
        center = w[2]
        dz.append(8.0 * (w[3] - w[1]) - (w[4] - w[0]))
        above, below = (0.0, others[c]) if side == 0 else (others[c], 0.0)
        p1 = pltpu.roll(jnp.where(r1, below, center), 7, 0)
        m1 = pltpu.roll(jnp.where(r7, above, center), 1, 0)
        p2 = pltpu.roll(jnp.where(r2, below, center), 6, 0)
        m2 = pltpu.roll(jnp.where(r6, above, center), 2, 0)
        dx.append(8.0 * (p1 - m1) - (p2 - m2))
        p1 = pltpu.roll(jnp.where(l1, rights[c], center), 127, 1)
        m1 = pltpu.roll(jnp.where(l7, lefts[c], center), 1, 1)
        p2 = pltpu.roll(jnp.where(l2, rights[c], center), 126, 1)
        m2 = pltpu.roll(jnp.where(l6, lefts[c], center), 2, 1)
        dy.append(8.0 * (p1 - m1) - (p2 - m2))
    return dz, dx, dy


def invariant(dz, dx, dy):
    cross = dz[1] * dx[0] + dz[2] * dy[0] + dx[2] * dy[1]
    return dz[0] * dz[0] + dx[1] * dx[1] + dy[2] * dy[2] + 2.0 * cross


def edge_terms(total, dz, dx, dy):
    return total, 2.0 * dz[1], 2.0 * dx[1], 2.0 * dy[1]


def middle_kernel(v_hbm, tab_ref, comp_ref, edge_ref, near_ref, far_ref, buf, sems):
    j = pl.program_id(0)

    def copy(k):
        lanes = pl.ds(pl.multiple_of(k * 128, 128), 128)
        inner = pl.ds(pl.multiple_of((k + 1) * 128, 128), 128)
        return pltpu.make_async_copy(v_hbm.at[:, :, :, lanes], buf.at[:, :, :, inner], sems.at[k])

    @pl.when(j == 0)
    def _():
        for k in range(8):
            copy(k).start()
        zeros = jnp.zeros((3, 32, 16, 128), F32)
        buf[:, :, :, 0:128] = zeros
        buf[:, :, :, 9 * 128 : 10 * 128] = zeros
        copy(0).wait()

    @pl.when(j < 7)
    def _():
        copy(j + 1).wait()

    masks = edge_masks()
    left = pl.ds(pl.multiple_of(j * 128, 128), 128)
    mid = pl.ds(pl.multiple_of(j * 128 + 128, 128), 128)
    right = pl.ds(pl.multiple_of(j * 128 + 256, 128), 128)
    near_ref[...] = buf[:, 0:4, :, mid]
    far_ref[...] = buf[:, 28:32, :, mid]
    for side in range(2):
        rows = slice(8 * side, 8 * side + 8)
        others = slice(8 - 8 * side, 16 - 8 * side)
        zeros = jnp.zeros((8, 128), F32)
        carry = (zeros + 1.0, [zeros] * 3)
        lines = [[buf[c, i, rows, mid] for i in range(32)] for c in range(3)]
        for z in range(2, 30):
            quarter, zz = z // 8, z % 8
            dz, dx, dy = gradients(
                [lines[c][z - 2 : z + 3] for c in range(3)],
                [buf[c, z, others, mid] for c in range(3)],
                [buf[c, z, rows, left] for c in range(3)],
                [buf[c, z, rows, right] for c in range(3)],
                side,
                masks,
            )
            total = invariant(dz, dx, dy)
            ends = slice(6 * side, 6 * side + 2)
            for e, value in enumerate(edge_terms(total, dz, dx, dy)):
                edge_ref[e, side, zz, 2 * quarter : 2 * quarter + 2, :] = value[ends]
            step, colors = lookup(QSCALE * total, tab_ref)
            carry = composite(carry, step, colors)
        for c in range(3):
            comp_ref[c, rows, :] = carry[1][c]
        comp_ref[3, rows, :] = carry[0]


def middle_pass(velocity, table):
    comps, depth, width, length = velocity.shape
    image = pl.BlockSpec((4, width, 128), lambda j: (0, 0, j))
    return pl.pallas_call(
        middle_kernel,
        grid=(8,),
        in_specs=[pl.BlockSpec(memory_space=pl.ANY), pl.BlockSpec((16, 8, 128), lambda j: (0, 0, 0))],
        out_specs=[
            image,
            pl.BlockSpec((4, 2, 8, 8, 128), lambda j: (0, 0, 0, 0, j)),
            pl.BlockSpec((comps, 4, width, 128), lambda j: (0, 0, 0, j)),
            pl.BlockSpec((comps, 4, width, 128), lambda j: (0, 0, 0, j)),
        ],
        out_shape=[
            jax.ShapeDtypeStruct((4, width, length), F32),
            jax.ShapeDtypeStruct((4, 2, 8, 8, length), F32),
            jax.ShapeDtypeStruct((comps, 4, width, length), F32),
            jax.ShapeDtypeStruct((comps, 4, width, length), F32),
        ],
        scratch_shapes=[pltpu.VMEM((comps, depth, width, length + 256), F32), pltpu.SemaphoreType.DMA((8,))],
        compiler_params=pltpu.CompilerParams(vmem_limit_bytes=VMEM_ALL),
        cost_estimate=pl.CostEstimate(flops=60000000, bytes_accessed=10000000, transcendentals=1000000),
        name="middle_pass",
    )(velocity, table)


def ends_kernel(near_ref, far_ref, zlo_ref, zhi_ref, comp_ref, tab_ref, out_ref, edge_ref):
    masks = edge_masks()
    zeros = jnp.zeros((8, 128), F32)
    for j in range(8):
        lanes = slice(j * 128, j * 128 + 128)
        for side in range(2):
            rows = slice(8 * side, 8 * side + 8)
            others = slice(8 - 8 * side, 16 - 8 * side)
            carry = (zeros + 1.0, [zeros] * 3)
            for k, block_ref in enumerate((near_ref, far_ref)):
                first = [[zlo_ref[c, i, rows, lanes] for i in range(2)] for c in range(3)] if k == 0 else [[]] * 3
                last = [[zhi_ref[c, i, rows, lanes] for i in range(2)] for c in range(3)] if k == 1 else [[]] * 3
                lines = [first[c] + [block_ref[c, i, rows, lanes] for i in range(4)] + last[c] for c in range(3)]
                for i in range(2):
                    at = i + 2 * k
                    sideways = lambda m: [
                        block_ref[c, at, rows, m * 128 : m * 128 + 128] if 0 <= m < 8 else zeros for c in range(3)
                    ]
                    dz, dx, dy = gradients(
                        [lines[c][i : i + 5] for c in range(3)],
                        [block_ref[c, at, others, lanes] for c in range(3)],
                        sideways(j - 1),
                        sideways(j + 1),
                        side,
                        masks,
                    )
                    total = invariant(dz, dx, dy)
                    ends = slice(6 * side, 6 * side + 2)
                    for e, value in enumerate(edge_terms(total, dz, dx, dy)):
                        edge_ref[e, side, i, 6 * k : 6 * k + 2, lanes] = value[ends]
                    step, colors = lookup(QSCALE * total, tab_ref)
                    carry = composite(carry, step, colors)
                if k == 0:
                    trans, shades = carry
                    shades = [s + trans * comp_ref[c, rows, lanes] for c, s in enumerate(shades)]
                    carry = (trans * comp_ref[3, rows, lanes], shades)
            for c in range(3):
                out_ref[c, rows, lanes] = carry[1][c]
            out_ref[3, rows, lanes] = carry[0]


def ends_pass(near, far, before, after, comp, table):
    width, length = comp.shape[1:]
    return pl.pallas_call(
        ends_kernel,
        out_shape=[
            jax.ShapeDtypeStruct((4, width, length), F32),
            jax.ShapeDtypeStruct((4, 2, 2, 8, length), F32),
        ],
        compiler_params=pltpu.CompilerParams(vmem_limit_bytes=VMEM_LIMIT),
        cost_estimate=pl.CostEstimate(flops=8000000, bytes_accessed=3000000, transcendentals=130000),
        name="ends_pass",
    )(near, far, before, after, comp, table)


def edge_kernel(edge_ref, ends_ref, lo_ref, hi_ref, comp_ref, tab_ref, mine_ref, other_ref):
    row = lax.broadcasted_iota(jnp.int32, (8, 128), 0)
    first, last = row < 2, row > 5
    core = lax.rem(lax.axis_index("depth"), 2)
    for slot, out_ref in enumerate((mine_ref, other_ref)):
        for k in range(4):
            piece = 2 * k + lax.rem(core + slot, 2)
            lanes = pl.ds(pl.multiple_of(piece * 128, 128), 128)
            out_ref[k] = comp_ref[:, :, lanes]
            for side, halo_ref in enumerate((lo_ref, hi_ref)):
                zeros = jnp.zeros((8, 128), F32)
                carry = (zeros + 1.0, [zeros] * 3)
                for zz in range(8):
                    terms = [edge_ref[e, side, zz, :, lanes] for e in range(4)]
                    if zz < 2:
                        terms = [jnp.where(first, ends_ref[e, side, zz, :, lanes], t) for e, t in enumerate(terms)]
                    if zz > 5:
                        terms = [jnp.where(last, ends_ref[e, side, zz - 6, :, lanes], t) for e, t in enumerate(terms)]
                    part, by_z, by_x, by_y = terms
                    hz, hx, hy = [halo_ref[c, zz, :, lanes] for c in range(3)]
                    total = part + by_z * hz + by_y * hy + hx * (by_x + hx)
                    step, colors = lookup(QSCALE * total, tab_ref)
                    carry = composite(carry, step, colors)
                trans, shades = carry
                for back in (2, 4):
                    shades = [s + trans * pltpu.roll(s, 8 - back, 0) for s in shades]
                    trans = trans * pltpu.roll(trans, 8 - back, 0)
                start = 14 * side
                for c in range(3):
                    out_ref[k, c, start : start + 2, :] = shades[c][0:2]
                out_ref[k, 3, start : start + 2, :] = trans[0:2]


def edge_pass(edge, ends, lo, hi, comp, table):
    pieces = jax.ShapeDtypeStruct((4, 4, comp.shape[1], 128), F32)
    return pl.pallas_call(
        edge_kernel,
        out_shape=[pieces, pieces],
        compiler_params=pltpu.CompilerParams(vmem_limit_bytes=VMEM_LIMIT),
        cost_estimate=pl.CostEstimate(flops=10000000, bytes_accessed=4000000, transcendentals=300000),
        name="edge_pass",
    )(edge, ends, lo, hi, comp, table)


def over(front, back):
    shade = front[..., :3, :, :] + front[..., 3:, :, :] * back[..., :3, :, :]
    return jnp.concatenate([shade, front[..., 3:, :, :] * back[..., 3:, :, :]], axis=-3)


def gather_over(mine, other):
    place = lax.axis_index("depth")
    core, chip = lax.rem(place, 2), lax.div(place, 2)
    got = lax.ppermute(other, "depth", [(i, i ^ 1) for i in range(8)])
    near = core == 0
    pair = over(jnp.where(near, mine, got), jnp.where(near, got, mine))
    parts = [lax.dynamic_index_in_dim(pair, chip, 0, keepdims=False)]
    for k in range(1, 4):
        piece = lax.dynamic_index_in_dim(pair, lax.rem(chip + k, 4), 0, keepdims=False)
        parts.append(lax.ppermute(piece, "depth", ring(8, 2 * k)))
    parts = jnp.stack(parts)
    result = lax.dynamic_index_in_dim(parts, lax.rem(chip + 1, 4), 0, keepdims=False)
    for source in (2, 1, 0):
        result = over(lax.dynamic_index_in_dim(parts, lax.rem(chip + 4 - source, 4), 0, keepdims=False), result)
    return result


def make_table(sigma_table, color_table, depth_total):
    values = jnp.concatenate([sigma_table[None] * (-1.0 / depth_total), color_table], axis=0)
    slopes = values[:, 1:] - values[:, :-1]
    starts = values[:, :-1] - slopes * jnp.arange(15, dtype=F32)
    table = jnp.concatenate([starts, slopes], axis=0)
    table = jnp.pad(table, ((0, 0), (0, 1))).reshape(16, 8, 1)
    return jnp.broadcast_to(table, (16, 8, 128))


def local(velocity, sigma_table, color_table):
    layers, tiles = lax.axis_size("depth"), lax.axis_size("tile")
    table = make_table(sigma_table, color_table, velocity.shape[1] * layers)
    up, down, zup, zdown = pack(velocity)
    lo = lax.ppermute(up, "tile", ring(tiles, 1))
    hi = lax.ppermute(down, "tile", ring(tiles, -1))
    before = lax.ppermute(zup, "depth", ring(layers, 1))
    after = lax.ppermute(zdown, "depth", ring(layers, -1))
    comp, edge, near, far = middle_pass(velocity, table)
    comp, ends = ends_pass(near, far, before, after, comp, table)
    mine, other = edge_pass(edge, ends, lo, hi, comp, table)
    return gather_over(mine, other)


def solution(mesh):
    return jax.shard_map(
        local,
        mesh=mesh,
        in_specs=(P(None, "depth", "tile", None), P(), P()),
        out_specs=P(None, "tile", "depth"),
        check_vma=False,
    )
```

```python
import jax
import jax.numpy as jnp
from jax import lax
from jax.experimental import pallas as pl
from jax.experimental.pallas import tpu as pltpu
from jax.sharding import PartitionSpec as P

F32 = jnp.float32
VMEM_LIMIT = 40 * 1024 * 1024
VMEM_ALL = 50 * 1024 * 1024
QSCALE = -1.0 / 1152.0


def ring(count, by):
    return [(i, (i + by) % count) for i in range(count)]


def pack_kernel(v_hbm, up_ref, down_ref, zup_ref, zdown_ref, buf, sems):
    copies = [
        [pltpu.make_async_copy(v_hbm.at[c, 8 * q : 8 * q + 8], buf.at[c, 8 * q : 8 * q + 8], sems.at[c, q]) for q in range(4)]
        for c in range(3)
    ]
    for some in copies:
        for copy in some:
            copy.start()
    tile, tiles = lax.axis_index("tile"), lax.axis_size("tile")
    layer, layers = lax.axis_index("depth"), lax.axis_size("depth")
    keep_up = jnp.where(tile == tiles - 1, 0.0, 1.0)
    keep_down = jnp.where(tile == 0, 0.0, 1.0)
    keep_zup = jnp.where(layer == layers - 1, 0.0, 1.0)
    keep_zdown = jnp.where(layer == 0, 0.0, 1.0)
    row = lax.broadcasted_iota(jnp.int32, (8, 1024), 0)
    for c in range(3):
        for quarter in range(4):
            copies[c][quarter].wait()
            for zz in range(8):
                z = quarter * 8 + zz
                low = buf[c, z, 0:8, :]
                high = buf[c, z, 8:16, :]
                up = jnp.where(row == 6, high - 8.0 * pltpu.roll(high, 7, 0), high)
                down = jnp.where(row == 0, -low, 8.0 * pltpu.roll(low, 1, 0) - low)
                up_ref[c, zz, 2 * quarter : 2 * quarter + 2, :] = keep_up * up[6:8]
                down_ref[c, zz, 2 * quarter : 2 * quarter + 2, :] = keep_down * down[0:2]
        zdown_ref[c] = keep_zdown * buf[c, 0:2]
        zup_ref[c] = keep_zup * buf[c, 30:32]


def pack(velocity):
    comps, depth, width, length = velocity.shape
    ends = jax.ShapeDtypeStruct((comps, 8, 8, length), F32)
    layers = jax.ShapeDtypeStruct((comps, 2, width, length), F32)
    return pl.pallas_call(
        pack_kernel,
        in_specs=[pl.BlockSpec(memory_space=pl.ANY)],
        out_shape=[ends, ends, layers, layers],
        scratch_shapes=[pltpu.VMEM((comps, depth, width, length), F32), pltpu.SemaphoreType.DMA((comps, 4))],
        compiler_params=pltpu.CompilerParams(vmem_limit_bytes=VMEM_ALL),
        cost_estimate=pl.CostEstimate(flops=2000000, bytes_accessed=9000000, transcendentals=0),
        name="pack",
    )(velocity)


def lookup(qcrit, tab_ref):
    pos = 7.5 * jnp.tanh(qcrit) + 7.5
    index = jnp.minimum(pos.astype(jnp.int32), 14)
    low, index = index < 8, index & 7
    pick = lambda k: jnp.take_along_axis(tab_ref[k], index, axis=0, mode="promise_in_bounds")
    base = [jnp.where(low, pick(2 * k), pick(2 * k + 1)) for k in range(8)]
    vals = [base[k] + base[k + 4] * pos for k in range(4)]
    return jnp.exp(vals[0]), vals[1:]


def composite(carry, step, colors):
    trans, shades = carry
    after = trans * step
    weight = trans - after
    return after, [s + weight * c for s, c in zip(shades, colors)]


def edge_masks():
    row = lax.broadcasted_iota(jnp.int32, (8, 128), 0)
    lane = lax.broadcasted_iota(jnp.int32, (8, 128), 1)
    return (row < 1, row > 6, row < 2, row > 5), (lane < 1, lane > 126, lane < 2, lane > 125)


def gradients(window, others, lefts, rights, side, masks):
    (r1, r7, r2, r6), (l1, l7, l2, l6) = masks
    dz, dx, dy = [], [], []
    for c in range(3):
        w = window[c]
        center = w[2]
        dz.append(8.0 * (w[3] - w[1]) - (w[4] - w[0]))
        above, below = (0.0, others[c]) if side == 0 else (others[c], 0.0)
        p1 = pltpu.roll(jnp.where(r1, below, center), 7, 0)
        m1 = pltpu.roll(jnp.where(r7, above, center), 1, 0)
        p2 = pltpu.roll(jnp.where(r2, below, center), 6, 0)
        m2 = pltpu.roll(jnp.where(r6, above, center), 2, 0)
        dx.append(8.0 * (p1 - m1) - (p2 - m2))
        p1 = pltpu.roll(jnp.where(l1, rights[c], center), 127, 1)
        m1 = pltpu.roll(jnp.where(l7, lefts[c], center), 1, 1)
        p2 = pltpu.roll(jnp.where(l2, rights[c], center), 126, 1)
        m2 = pltpu.roll(jnp.where(l6, lefts[c], center), 2, 1)
        dy.append(8.0 * (p1 - m1) - (p2 - m2))
    return dz, dx, dy


def invariant(dz, dx, dy):
    cross = dz[1] * dx[0] + dz[2] * dy[0] + dx[2] * dy[1]
    return dz[0] * dz[0] + dx[1] * dx[1] + dy[2] * dy[2] + 2.0 * cross


def edge_terms(total, dz, dx, dy):
    return total, 2.0 * dz[1], 2.0 * dx[1], 2.0 * dy[1]


def middle_kernel(v_hbm, tab_ref, comp_ref, edge_ref, near_ref, far_ref, buf, sems):
    j = pl.program_id(0)

    def copy(k):
        lanes = pl.ds(pl.multiple_of(k * 128, 128), 128)
        inner = pl.ds(pl.multiple_of((k + 1) * 128, 128), 128)
        return pltpu.make_async_copy(v_hbm.at[:, :, :, lanes], buf.at[:, :, :, inner], sems.at[k])

    @pl.when(j == 0)
    def _():
        for k in range(8):
            copy(k).start()
        zeros = jnp.zeros((3, 32, 16, 128), F32)
        buf[:, :, :, 0:128] = zeros
        buf[:, :, :, 9 * 128 : 10 * 128] = zeros
        copy(0).wait()

    @pl.when(j < 7)
    def _():
        copy(j + 1).wait()

    masks = edge_masks()
    left = pl.ds(pl.multiple_of(j * 128, 128), 128)
    mid = pl.ds(pl.multiple_of(j * 128 + 128, 128), 128)
    right = pl.ds(pl.multiple_of(j * 128 + 256, 128), 128)
    near_ref[...] = buf[:, 0:4, :, mid]
    far_ref[...] = buf[:, 28:32, :, mid]
    for side in range(2):
        rows = slice(8 * side, 8 * side + 8)
        others = slice(8 - 8 * side, 16 - 8 * side)
        zeros = jnp.zeros((8, 128), F32)
        carry = (zeros + 1.0, [zeros] * 3)
        lines = [[buf[c, i, rows, mid] for i in range(32)] for c in range(3)]
        for z in range(2, 30):
            quarter, zz = z // 8, z % 8
            dz, dx, dy = gradients(
                [lines[c][z - 2 : z + 3] for c in range(3)],
                [buf[c, z, others, mid] for c in range(3)],
                [buf[c, z, rows, left] for c in range(3)],
                [buf[c, z, rows, right] for c in range(3)],
                side,
                masks,
            )
            total = invariant(dz, dx, dy)
            ends = slice(6 * side, 6 * side + 2)
            for e, value in enumerate(edge_terms(total, dz, dx, dy)):
                edge_ref[e, side, zz, 2 * quarter : 2 * quarter + 2, :] = value[ends]
            step, colors = lookup(QSCALE * total, tab_ref)
            carry = composite(carry, step, colors)
        for c in range(3):
            comp_ref[c, rows, :] = carry[1][c]
        comp_ref[3, rows, :] = carry[0]


def middle_pass(velocity, table):
    comps, depth, width, length = velocity.shape
    image = pl.BlockSpec((4, width, 128), lambda j: (0, 0, j))
    return pl.pallas_call(
        middle_kernel,
        grid=(8,),
        in_specs=[pl.BlockSpec(memory_space=pl.ANY), pl.BlockSpec((16, 8, 128), lambda j: (0, 0, 0))],
        out_specs=[
            image,
            pl.BlockSpec((4, 2, 8, 8, 128), lambda j: (0, 0, 0, 0, j)),
            pl.BlockSpec((comps, 4, width, 128), lambda j: (0, 0, 0, j)),
            pl.BlockSpec((comps, 4, width, 128), lambda j: (0, 0, 0, j)),
        ],
        out_shape=[
            jax.ShapeDtypeStruct((4, width, length), F32),
            jax.ShapeDtypeStruct((4, 2, 8, 8, length), F32),
            jax.ShapeDtypeStruct((comps, 4, width, length), F32),
            jax.ShapeDtypeStruct((comps, 4, width, length), F32),
        ],
        scratch_shapes=[pltpu.VMEM((comps, depth, width, length + 256), F32), pltpu.SemaphoreType.DMA((8,))],
        compiler_params=pltpu.CompilerParams(vmem_limit_bytes=VMEM_ALL),
        cost_estimate=pl.CostEstimate(flops=60000000, bytes_accessed=10000000, transcendentals=1000000),
        name="middle_pass",
    )(velocity, table)


def ends_kernel(near_ref, far_ref, zlo_ref, zhi_ref, comp_ref, tab_ref, out_ref, edge_ref):
    masks = edge_masks()
    zeros = jnp.zeros((8, 128), F32)
    for j in range(8):
        lanes = slice(j * 128, j * 128 + 128)
        for side in range(2):
            rows = slice(8 * side, 8 * side + 8)
            others = slice(8 - 8 * side, 16 - 8 * side)
            carry = (zeros + 1.0, [zeros] * 3)
            for k, block_ref in enumerate((near_ref, far_ref)):
                first = [[zlo_ref[c, i, rows, lanes] for i in range(2)] for c in range(3)] if k == 0 else [[]] * 3
                last = [[zhi_ref[c, i, rows, lanes] for i in range(2)] for c in range(3)] if k == 1 else [[]] * 3
                lines = [first[c] + [block_ref[c, i, rows, lanes] for i in range(4)] + last[c] for c in range(3)]
                for i in range(2):
                    at = i + 2 * k
                    sideways = lambda m: [
                        block_ref[c, at, rows, m * 128 : m * 128 + 128] if 0 <= m < 8 else zeros for c in range(3)
                    ]
                    dz, dx, dy = gradients(
                        [lines[c][i : i + 5] for c in range(3)],
                        [block_ref[c, at, others, lanes] for c in range(3)],
                        sideways(j - 1),
                        sideways(j + 1),
                        side,
                        masks,
                    )
                    total = invariant(dz, dx, dy)
                    ends = slice(6 * side, 6 * side + 2)
                    for e, value in enumerate(edge_terms(total, dz, dx, dy)):
                        edge_ref[e, side, i, 6 * k : 6 * k + 2, lanes] = value[ends]
                    step, colors = lookup(QSCALE * total, tab_ref)
                    carry = composite(carry, step, colors)
                if k == 0:
                    trans, shades = carry
                    shades = [s + trans * comp_ref[c, rows, lanes] for c, s in enumerate(shades)]
                    carry = (trans * comp_ref[3, rows, lanes], shades)
            for c in range(3):
                out_ref[c, rows, lanes] = carry[1][c]
            out_ref[3, rows, lanes] = carry[0]


def ends_pass(near, far, before, after, comp, table):
    width, length = comp.shape[1:]
    return pl.pallas_call(
        ends_kernel,
        out_shape=[
            jax.ShapeDtypeStruct((4, width, length), F32),
            jax.ShapeDtypeStruct((4, 2, 2, 8, length), F32),
        ],
        compiler_params=pltpu.CompilerParams(vmem_limit_bytes=VMEM_LIMIT),
        cost_estimate=pl.CostEstimate(flops=8000000, bytes_accessed=3000000, transcendentals=130000),
        name="ends_pass",
    )(near, far, before, after, comp, table)


def edge_kernel(edge_ref, ends_ref, lo_ref, hi_ref, comp_ref, tab_ref, mine_ref, other_ref):
    row = lax.broadcasted_iota(jnp.int32, (8, 128), 0)
    first, last = row < 2, row > 5
    core = lax.rem(lax.axis_index("depth"), 2)
    for slot, out_ref in enumerate((mine_ref, other_ref)):
        for k in range(4):
            piece = 2 * k + lax.rem(core + slot, 2)
            lanes = pl.ds(pl.multiple_of(piece * 128, 128), 128)
            out_ref[k] = comp_ref[:, :, lanes]
            for side, halo_ref in enumerate((lo_ref, hi_ref)):
                zeros = jnp.zeros((8, 128), F32)
                carry = (zeros + 1.0, [zeros] * 3)
                for zz in range(8):
                    terms = [edge_ref[e, side, zz, :, lanes] for e in range(4)]
                    if zz < 2:
                        terms = [jnp.where(first, ends_ref[e, side, zz, :, lanes], t) for e, t in enumerate(terms)]
                    if zz > 5:
                        terms = [jnp.where(last, ends_ref[e, side, zz - 6, :, lanes], t) for e, t in enumerate(terms)]
                    part, by_z, by_x, by_y = terms
                    hz, hx, hy = [halo_ref[c, zz, :, lanes] for c in range(3)]
                    total = part + by_z * hz + by_y * hy + hx * (by_x + hx)
                    step, colors = lookup(QSCALE * total, tab_ref)
                    carry = composite(carry, step, colors)
                trans, shades = carry
                for back in (2, 4):
                    shades = [s + trans * pltpu.roll(s, 8 - back, 0) for s in shades]
                    trans = trans * pltpu.roll(trans, 8 - back, 0)
                start = 14 * side
                for c in range(3):
                    out_ref[k, c, start : start + 2, :] = shades[c][0:2]
                out_ref[k, 3, start : start + 2, :] = trans[0:2]


def edge_pass(edge, ends, lo, hi, comp, table):
    pieces = jax.ShapeDtypeStruct((4, 4, comp.shape[1], 128), F32)
    return pl.pallas_call(
        edge_kernel,
        out_shape=[pieces, pieces],
        compiler_params=pltpu.CompilerParams(vmem_limit_bytes=VMEM_LIMIT),
        cost_estimate=pl.CostEstimate(flops=10000000, bytes_accessed=4000000, transcendentals=300000),
        name="edge_pass",
    )(edge, ends, lo, hi, comp, table)


def over(front, back):
    shade = front[..., :3, :, :] + front[..., 3:, :, :] * back[..., :3, :, :]
    return jnp.concatenate([shade, front[..., 3:, :, :] * back[..., 3:, :, :]], axis=-3)


def gather_over(mine, other):
    place = lax.axis_index("depth")
    core, chip = lax.rem(place, 2), lax.div(place, 2)
    got = lax.ppermute(other, "depth", [(i, i ^ 1) for i in range(8)])
    near = core == 0
    pair = over(jnp.where(near, mine, got), jnp.where(near, got, mine))
    parts = [lax.dynamic_index_in_dim(pair, chip, 0, keepdims=False)]
    for k in range(1, 4):
        piece = lax.dynamic_index_in_dim(pair, lax.rem(chip + k, 4), 0, keepdims=False)
        parts.append(lax.ppermute(piece, "depth", ring(8, 2 * k)))
    def at(source):
        turn = lax.rem(chip + 4 - source, 4)
        return jnp.where(turn < 2, jnp.where(turn == 0, parts[0], parts[1]), jnp.where(turn == 2, parts[2], parts[3]))

    result = at(3)
    for source in (2, 1, 0):
        result = over(at(source), result)
    return result


def make_table(sigma_table, color_table, depth_total):
    values = jnp.concatenate([sigma_table[None] * (-1.0 / depth_total), color_table], axis=0)
    slopes = values[:, 1:] - values[:, :-1]
    starts = values[:, :-1] - slopes * jnp.arange(15, dtype=F32)
    table = jnp.concatenate([starts, slopes], axis=0)
    table = jnp.pad(table, ((0, 0), (0, 1))).reshape(16, 8, 1)
    return jnp.broadcast_to(table, (16, 8, 128))


def local(velocity, sigma_table, color_table):
    layers, tiles = lax.axis_size("depth"), lax.axis_size("tile")
    table = make_table(sigma_table, color_table, velocity.shape[1] * layers)
    up, down, zup, zdown = pack(velocity)
    lo = lax.ppermute(up, "tile", ring(tiles, 1))
    hi = lax.ppermute(down, "tile", ring(tiles, -1))
    before = lax.ppermute(zup, "depth", ring(layers, 1))
    after = lax.ppermute(zdown, "depth", ring(layers, -1))
    comp, edge, near, far = middle_pass(velocity, table)
    comp, ends = ends_pass(near, far, before, after, comp, table)
    mine, other = edge_pass(edge, ends, lo, hi, comp, table)
    return gather_over(mine, other)


def solution(mesh):
    return jax.shard_map(
        local,
        mesh=mesh,
        in_specs=(P(None, "depth", "tile", None), P(), P()),
        out_specs=P(None, "tile", "depth"),
        check_vma=False,
    )
```
